512 devices in a mesh: scan: 16 (over x, y_hi, core), depth: 32 (over z, y_lo).
Axes of the slice: x: 4, y: 4 (y_hi: 2, y_lo: 2; y = y_hi * 2 + y_lo), z: 16, core: 2. Of those that a mesh axis runs over, the one named last changes fastest.
Arguments:
- phase: float32 [32, 384, 384], P('depth'), may hold values from -3.140625 to 3.140625
- absorb: float32 [32, 384, 384], P('depth'), may hold values from 0 to 0.1
- probe: float32 [2, 128, 128], replicated, may hold values from -6 to 6
- offsets: int32 [128, 2], P('scan'), may hold values from 0 to 256
- measured: float32 [128, 128, 128], P('scan'), may hold values from 0 to 2
Outputs:
- grad_phase: float32 [32, 384, 384], P('depth', 'scan')
- grad_absorb: float32 [32, 384, 384], P('depth', 'scan')
The draws below stay inside these ranges and needn't reach their ends.
All inputs are finite; a program needn't handle non-finite values.
Results may differ from the reference program's by a relative error of at most 0.0003.
Values sent between devices are 32-bit elements; how exact they have to be, the bound alone decides.
A program may use at most 64 MiB of HBM per device.

```python
import math
import jax
import jax.numpy as jnp
from jax import lax

WIN = 128
OBJ = 384
SLICES = 32
POSITIONS = 128


def set_ends(result, rng, smallest, largest):
    dims = result.shape
    spot = [jax.random.randint(jax.random.fold_in(rng, axis), (), 0, dims[axis]) for axis in range(len(dims))]
    result = result.at[tuple(spot)].set(smallest)
    longest = dims.index(max(dims))
    spot[longest] = (spot[longest] + 1) % dims[longest]
    return result.at[tuple(spot)].set(largest)


def level_of(own_key, dims, pieces, smallest, top_value):
    gain = 1.0
    for dim, shards_of in pieces:
        steps = jax.random.uniform(jax.random.fold_in(jax.random.fold_in(own_key, 6), dim), (shards_of,), jnp.float32, smallest / len(pieces), top_value / len(pieces))
        gain = gain * jnp.repeat(jnp.exp(steps), dims[dim] // shards_of).reshape((-1,) + (1,) * (len(dims) - 1 - dim))
    return gain


def noise(own_key, extent, width, reach, kind=jnp.bfloat16):
    return jnp.clip(width * jax.random.normal(own_key, extent, jnp.float32), -reach, reach).astype(kind)


def setup_inputs(seed: int = 0) -> dict:
    arg_keys = jax.random.split(jax.random.key(seed), 6)
    phase = jnp.clip(jax.random.uniform(arg_keys[0], (SLICES, OBJ, OBJ), jnp.float32, -3.140625, 3.140625), -3.140625, 3.140625)
    absorb = jnp.clip(0.1 * jax.random.uniform(arg_keys[1], (SLICES, OBJ, OBJ), jnp.float32) ** level_of(arg_keys[1], (SLICES, OBJ, OBJ), ((0, 32),), -0.2, 0.2), 0.0, 0.1)
    probe = noise(arg_keys[2], (2, WIN, WIN), 1.0, 6.0, jnp.float32)
    offsets = set_ends(jax.random.randint(arg_keys[3], (POSITIONS, 2), 0, OBJ - WIN + 1), jax.random.fold_in(arg_keys[3], 1), 0, OBJ - WIN).astype(jnp.int32)
    measured = jnp.clip(2.0 * jax.random.uniform(arg_keys[4], (POSITIONS, WIN, WIN), jnp.float32) ** level_of(arg_keys[4], (POSITIONS, WIN, WIN), ((0, 16),), -0.2, 0.2), 0.0, 2.0)
    return dict(phase=phase, absorb=absorb, probe=probe, offsets=offsets, measured=measured)


chirp_rate = 1.0
highest = lax.Precision.HIGHEST

def dft_table(win_size, sign):
    indices = jnp.arange(win_size, dtype=jnp.int32)
    products = indices[:, None] * indices[None, :] % win_size
    angles = 2.0 * math.pi / win_size * products.astype(jnp.float32)
    norm_scale = 1.0 / math.sqrt(win_size)
    real_part = jnp.cos(angles) * norm_scale
    imag_part = sign * jnp.sin(angles) * norm_scale
    return jnp.stack([jnp.stack([real_part, imag_part]), jnp.stack([-imag_part, real_part])])

def propagator(win_size):
    indices = jnp.arange(win_size, dtype=jnp.int32)
    signed = jnp.where(indices < win_size // 2, indices, indices - win_size).astype(jnp.float32)
    radius = signed[:, None] ** 2 + signed[None, :] ** 2
    angles = -chirp_rate * radius / win_size
    return jnp.stack([jnp.cos(angles), jnp.sin(angles)])

def complex_mul(first, second):
    return jnp.stack([first[0] * second[0] - first[1] * second[1], first[0] * second[1] + first[1] * second[0]])

def complex_conj(values):
    return jnp.stack([values[0], -values[1]])

def transform(values, table):
    half_done = jnp.einsum('cij,cdjk->dik', values, table, precision=highest)
    return jnp.einsum('cdij,cjk->dik', table, half_done, precision=highest)

def reference(phase, absorb, probe, offsets, measured):
    win_size = probe.shape[-1]
    slices = phase.shape[0]
    obj_size = phase.shape[1]
    fwd_table = dft_table(win_size, -1.0)
    inv_table = dft_table(win_size, 1.0)
    prop_filt = propagator(win_size)
    back_filt = complex_conj(prop_filt)

    def one_position(gradients, position_data):
        offset_pair, target = position_data
        row_off = offset_pair[0].astype(jnp.int32)
        col_off = offset_pair[1].astype(jnp.int32)
        zero_idx = jnp.int32(0)
        phase_win = lax.dynamic_slice(phase, (zero_idx, row_off, col_off), (slices, win_size, win_size))
        absorb_win = lax.dynamic_slice(absorb, (zero_idx, row_off, col_off), (slices, win_size, win_size))
        amplitude = jnp.exp(-absorb_win)
        trans_all = jnp.stack([amplitude * jnp.cos(phase_win), amplitude * jnp.sin(phase_win)], axis=1)

        def forward(wave_in, trans_win):
            exit_wave = complex_mul(wave_in, trans_win)
            onward = transform(complex_mul(prop_filt, transform(exit_wave, fwd_table)), inv_table)
            return (onward, exit_wave)
        _, exit_stack = lax.scan(forward, probe, trans_all)
        far_field = transform(exit_stack[-1], fwd_table)
        residual = far_field[0] ** 2 + far_field[1] ** 2 - target
        adjoint_last = transform(residual[None] * far_field, inv_table)

        def backward(adjoint, pair_data):
            exit_wave, trans_win = pair_data
            prod_re = exit_wave[0] * adjoint[0] + exit_wave[1] * adjoint[1]
            prod_im = exit_wave[0] * adjoint[1] - exit_wave[1] * adjoint[0]
            earlier = transform(complex_mul(back_filt, transform(complex_mul(complex_conj(trans_win), adjoint), fwd_table)), inv_table)
            return (earlier, jnp.stack([prod_im, -prod_re]))
        _, contrib = lax.scan(backward, adjoint_last, (exit_stack, trans_all), reverse=True)
        contrib = jnp.transpose(contrib, (1, 0, 2, 3))
        start = (zero_idx, zero_idx, row_off, col_off)
        grad_patch = lax.dynamic_slice(gradients, start, (2, slices, win_size, win_size))
        gradients = lax.dynamic_update_slice(gradients, grad_patch + contrib, start)
        return (gradients, None)
    gradients = jnp.zeros((2, slices, obj_size, obj_size), jnp.float32)
    gradients, _ = lax.scan(one_position, gradients, (offsets, measured))
    return (gradients[0], gradients[1])
```

```python
import functools

import jax
import jax.numpy as jnp
import ml_dtypes
import numpy as np
from jax import lax
from jax.experimental import pallas as pl
from jax.experimental.pallas import tpu as pltpu
from jax.sharding import PartitionSpec as P

MESH = pl.DeviceIdType.MESH
BF16 = jnp.bfloat16
F32 = jnp.float32
STRIDE = 4


def tables(win):
    idx = np.arange(win)
    ang = 2.0 * np.pi * (np.outer(idx, idx) % win) / win
    fwd = np.exp(-1j * ang) / np.sqrt(win)
    signed = np.where(idx < win // 2, idx, idx - win).astype(np.float64)
    chirp = np.exp(-1j * signed**2 / win)
    prop = np.conj(fwd) @ (chirp[:, None] * fwd)
    prop = 0.5 * (prop + prop.T)
    out = []
    for mat in (prop, fwd):
        right = np.block([[mat.real, mat.imag], [-mat.imag, mat.real]])
        left = np.block([[mat.real, -mat.imag], [mat.imag, mat.real]])
        for block in (right, left):
            block = block.astype(np.float32)
            high = block.astype(ml_dtypes.bfloat16)
            low = (block - high.astype(np.float32)).astype(ml_dtypes.bfloat16)
            out += [high, low]
    return np.stack(out)


def split(values):
    high = values.astype(BF16)
    low = (values - high.astype(F32)).astype(BF16)
    return high, low


def sandwich(re, im, tab, right, left):
    win = re.shape[0]
    high, low = split(jnp.concatenate([re, im], axis=1))
    both = jnp.concatenate([high, low], axis=0)
    main = jnp.dot(both, tab[right], preferred_element_type=F32)
    half = main[:win] + main[win:] + jnp.dot(high, tab[right + 1], preferred_element_type=F32)
    high, low = split(jnp.concatenate([half[:, :win], half[:, win:]], axis=0))
    both = jnp.concatenate([high, low], axis=1)
    main = jnp.dot(tab[left], both, preferred_element_type=F32)
    done = main[:, :win] + main[:, win:] + jnp.dot(tab[left + 1], high, preferred_element_type=F32)
    return done[:win], done[win:]


def window_kernel(off_ref, phase_ref, absorb_ref, out_ref, field):
    win = out_ref.shape[-1]
    obj = phase_ref.shape[-1]
    amp = jnp.exp(-absorb_ref[0])
    phase = phase_ref[0]
    field[0, :obj] = amp * jnp.cos(phase)
    field[1, :obj] = amp * jnp.sin(phase)

    def one(i, carry):
        row, col = off_ref[i, 0], off_ref[i, 1]
        high = lax.div(row, 8)
        low = row - 8 * high
        for part in range(2):
            rows = field[part, pl.ds(pl.multiple_of(8 * high, 8), win + 8), :]
            cols = pltpu.roll(rows, lax.rem(obj - col, obj), 1)[:, :win]
            out_ref[i, part] = pltpu.roll(cols, lax.rem(win + 8 - low, win + 8), 0)[:win]
        return carry

    lax.fori_loop(0, out_ref.shape[0], one, 0)


def field_kernel(off_ref, got_ref, out_ref, field):
    win = got_ref.shape[-1]
    obj = out_ref.shape[-1]
    field[...] = jnp.zeros_like(field)

    def one(i, carry):
        row, col = off_ref[i, 0], off_ref[i, 1]
        high = lax.div(row, 8)
        low = row - 8 * high
        for part in range(2):
            tall = jnp.concatenate([got_ref[i, part], jnp.zeros((8, win), F32)], axis=0)
            tall = pltpu.roll(tall, low, 0)
            wide = jnp.concatenate([tall, jnp.zeros((win + 8, obj - win), F32)], axis=1)
            field[part, pl.ds(pl.multiple_of(8 * high, 8), win + 8), :] += pltpu.roll(wide, col, 1)
        return carry

    lax.fori_loop(0, got_ref.shape[0], one, 0)
    out_ref[...] = field[:, :obj]


def chain_kernel(
    sections, num_pos, tw_ref, probe_ref, meas_ref, tab_ref, got_ref,
    trans, exits, wave, win_send, win_recv, grad_send, grad_recv,
):
    scan = lax.axis_index("scan")
    me = lax.axis_index("depth")
    shift = 3 * lax.rem(scan, 2)
    slot = lax.div(me + 4 - shift, STRIDE) - 1
    active = lax.rem(me + 4 - shift, STRIDE) == 0

    def home(i):
        return STRIDE * i + shift

    barrier = pltpu.get_barrier_semaphore()

    @pl.when(active)
    def _():
        def greet(d, carry):
            @pl.when(d != me)
            def _():
                pl.semaphore_signal(barrier, inc=1, device_id=(scan, d), device_id_type=MESH)
            return carry
        lax.fori_loop(0, sections, greet, 0)
        pl.semaphore_wait(barrier, sections - 1)

    @pl.when(jnp.logical_not(active))
    def _():
        def greet(i, carry):
            pl.semaphore_signal(barrier, inc=1, device_id=(scan, home(i)), device_id_type=MESH)
            return carry
        lax.fori_loop(0, num_pos, greet, 0)
        pl.semaphore_wait(barrier, num_pos)

    def window_copy(i):
        return pltpu.make_async_remote_copy(
            src_ref=tw_ref.at[i], dst_ref=trans.at[me], send_sem=win_send.at[i], recv_sem=win_recv.at[me],
            device_id=(scan, home(i)), device_id_type=MESH)

    def send_window(i, carry):
        @pl.when(home(i) != me)
        def _():
            window_copy(i).start()

        @pl.when(home(i) == me)
        def _():
            pltpu.make_async_copy(tw_ref.at[i], trans.at[me], win_recv.at[me]).start()
        return carry

    lax.fori_loop(0, num_pos, send_window, 0)

    def grad_copy(k):
        return pltpu.make_async_remote_copy(
            src_ref=exits.at[k], dst_ref=got_ref.at[slot], send_sem=grad_send.at[k], recv_sem=grad_recv.at[slot],
            device_id=(scan, k), device_id_type=MESH)

    @pl.when(active)
    def _():
        wave[...] = probe_ref[...]

        def step_in(k):
            pltpu.make_async_copy(tw_ref.at[0], trans.at[k], win_recv.at[k]).wait()
            tr, ti = trans[k, 0], trans[k, 1]
            wr, wi = wave[0], wave[1]
            er = wr * tr - wi * ti
            ei = wr * ti + wi * tr
            exits[k, 0] = er
            exits[k, 1] = ei
            return er, ei

        def forward(k, carry):
            er, ei = step_in(k)
            wr, wi = sandwich(er, ei, tab_ref, 0, 2)
            wave[0] = wr
            wave[1] = wi
            return carry

        lax.fori_loop(0, sections - 1, forward, 0)
        er, ei = step_in(sections - 1)
        fr, fi = sandwich(er, ei, tab_ref, 4, 6)
        resid = fr * fr + fi * fi - meas_ref[slot]
        lr, li = sandwich(resid * fr, resid * fi, tab_ref, 6, 4)
        wave[0] = lr
        wave[1] = li

        def grads(k):
            er, ei = exits[k, 0], exits[k, 1]
            lr, li = wave[0], wave[1]
            exits[k, 0] = er * li - ei * lr
            exits[k, 1] = -(er * lr + ei * li)

            @pl.when(k != me)
            def _():
                grad_copy(k).start()

            @pl.when(k == me)
            def _():
                pltpu.make_async_copy(exits.at[k], got_ref.at[slot], grad_recv.at[slot]).start()
            return lr, li

        def backward(j, carry):
            k = sections - 1 - j
            lr, li = grads(k)
            tr, ti = trans[k, 0], trans[k, 1]
            wr, wi = sandwich(tr * lr + ti * li, tr * li - ti * lr, tab_ref, 2, 0)
            wave[0] = wr
            wave[1] = wi
            return carry

        lax.fori_loop(0, sections - 1, backward, 0)
        grads(0)

    def finish(i, carry):
        @pl.when(home(i) != me)
        def _():
            window_copy(i).wait_send()
        pltpu.make_async_copy(tw_ref.at[0], got_ref.at[i], grad_recv.at[i]).wait()
        return carry

    lax.fori_loop(0, num_pos, finish, 0)

    @pl.when(active)
    def _():
        def drain(k, carry):
            @pl.when(k != me)
            def _():
                grad_copy(k).wait_send()
            return carry
        lax.fori_loop(0, sections, drain, 0)


def shards(tab, phase, absorb, probe, offsets, measured):
    win = probe.shape[-1]
    obj = phase.shape[-1]
    num_pos = offsets.shape[0]
    sections = lax.axis_size("depth")
    vmem = pl.BlockSpec(memory_space=pltpu.VMEM)
    smem = pl.BlockSpec(memory_space=pltpu.SMEM)
    limit = 48 * 1024 * 1024
    windows = pl.pallas_call(
        window_kernel,
        out_shape=jax.ShapeDtypeStruct((num_pos, 2, win, win), F32),
        in_specs=[smem, vmem, vmem],
        out_specs=vmem,
        scratch_shapes=[pltpu.VMEM((2, obj + 8, obj), F32)],
        compiler_params=pltpu.CompilerParams(vmem_limit_bytes=limit),
    )(offsets, phase, absorb)
    got = pl.pallas_call(
        functools.partial(chain_kernel, sections, num_pos),
        out_shape=jax.ShapeDtypeStruct((num_pos, 2, win, win), F32),
        in_specs=[vmem] * 4,
        out_specs=vmem,
        scratch_shapes=[
            pltpu.VMEM((sections, 2, win, win), F32),
            pltpu.VMEM((sections, 2, win, win), F32),
            pltpu.VMEM((2, win, win), F32),
            pltpu.SemaphoreType.DMA((num_pos,)),
            pltpu.SemaphoreType.DMA((sections,)),
            pltpu.SemaphoreType.DMA((sections,)),
            pltpu.SemaphoreType.DMA((num_pos,)),
        ],
        compiler_params=pltpu.CompilerParams(
            collective_id=0, has_side_effects=True, vmem_limit_bytes=limit),
    )(windows, probe, measured, tab)
    fields = pl.pallas_call(
        field_kernel,
        out_shape=jax.ShapeDtypeStruct((2, obj, obj), F32),
        in_specs=[smem, vmem],
        out_specs=vmem,
        scratch_shapes=[pltpu.VMEM((2, obj + 8, obj), F32)],
        compiler_params=pltpu.CompilerParams(vmem_limit_bytes=limit),
    )(offsets, got)
    reduced = lax.psum_scatter(fields, "scan", scatter_dimension=1, tiled=True)
    return reduced[0][None], reduced[1][None]


def solution(mesh):
    tab = tables(128)
    in_specs = (
        P("depth", None, None),
        P("depth", None, None),
        P(),
        P("scan", None),
        P("scan", None, None),
    )
    out_specs = (P("depth", "scan", None), P("depth", "scan", None))

    def run(phase, absorb, probe, offsets, measured):
        body = functools.partial(shards, jnp.asarray(tab))
        return jax.shard_map(body, mesh=mesh, in_specs=in_specs, out_specs=out_specs, check_vma=False)(
            phase, absorb, probe, offsets, measured)

    return run
```

```python
import functools

import jax
import jax.numpy as jnp
import ml_dtypes
import numpy as np
from jax import lax
from jax.experimental import pallas as pl
from jax.experimental.pallas import tpu as pltpu
from jax.sharding import PartitionSpec as P

MESH = pl.DeviceIdType.MESH
BF16 = jnp.bfloat16
F32 = jnp.float32
STRIDE = 4


def tables(win):
    idx = np.arange(win)
    ang = 2.0 * np.pi * (np.outer(idx, idx) % win) / win
    fwd = np.exp(-1j * ang) / np.sqrt(win)
    signed = np.where(idx < win // 2, idx, idx - win).astype(np.float64)
    chirp = np.exp(-1j * signed**2 / win)
    prop = np.conj(fwd) @ (chirp[:, None] * fwd)
    prop = 0.5 * (prop + prop.T)
    out = []
    for mat in (prop, fwd):
        right = np.block([[mat.real, mat.imag], [-mat.imag, mat.real]])
        left = np.block([[mat.real, -mat.imag], [mat.imag, mat.real]])
        for block in (right, left):
            block = block.astype(np.float32)
            high = block.astype(ml_dtypes.bfloat16)
            low = (block - high.astype(np.float32)).astype(ml_dtypes.bfloat16)
            out += [high, low]
    return np.stack(out)


def split(values):
    high = values.astype(BF16)
    low = (values - high.astype(F32)).astype(BF16)
    return high, low


def sandwich(re, im, tab, right, left):
    win = re.shape[0]
    high, low = split(jnp.concatenate([re, im], axis=1))
    both = jnp.concatenate([high, low], axis=0)
    main = jnp.dot(both, tab[right], preferred_element_type=F32)
    half = main[:win] + main[win:] + jnp.dot(high, tab[right + 1], preferred_element_type=F32)
    high, low = split(jnp.concatenate([half[:, :win], half[:, win:]], axis=0))
    both = jnp.concatenate([high, low], axis=1)
    main = jnp.dot(tab[left], both, preferred_element_type=F32)
    done = main[:, :win] + main[:, win:] + jnp.dot(tab[left + 1], high, preferred_element_type=F32)
    return done[:win], done[win:]


def window_kernel(off_ref, phase_ref, absorb_ref, out_ref, field):
    win = out_ref.shape[-1]
    obj = phase_ref.shape[-1]
    amp = jnp.exp(-absorb_ref[0])
    phase = phase_ref[0]
    field[0, :obj] = amp * jnp.cos(phase)
    field[1, :obj] = amp * jnp.sin(phase)

    def one(i, carry):
        row, col = off_ref[i, 0], off_ref[i, 1]
        high = lax.div(row, 8)
        low = row - 8 * high
        for part in range(2):
            rows = field[part, pl.ds(pl.multiple_of(8 * high, 8), win + 8), :]
            cols = pltpu.roll(rows, lax.rem(obj - col, obj), 1)[:, :win]
            out_ref[i, part] = pltpu.roll(cols, lax.rem(win + 8 - low, win + 8), 0)[:win]
        return carry

    lax.fori_loop(0, out_ref.shape[0], one, 0)


def field_kernel(off_ref, got_ref, out_ref, field):
    win = got_ref.shape[-1]
    obj = out_ref.shape[-1]
    field[...] = jnp.zeros_like(field)

    def one(i, carry):
        row, col = off_ref[i, 0], off_ref[i, 1]
        high = lax.div(row, 8)
        low = row - 8 * high
        for part in range(2):
            tall = jnp.concatenate([got_ref[i, part], jnp.zeros((8, win), F32)], axis=0)
            tall = pltpu.roll(tall, low, 0)
            wide = jnp.concatenate([tall, jnp.zeros((win + 8, obj - win), F32)], axis=1)
            field[part, pl.ds(pl.multiple_of(8 * high, 8), win + 8), :] += pltpu.roll(wide, col, 1)
        return carry

    lax.fori_loop(0, got_ref.shape[0], one, 0)
    out_ref[...] = field[:, :obj]


def chain_kernel(
    sections, num_pos, tw_ref, probe_ref, meas_ref, tab_ref, got_ref,
    trans, exits, wave, win_send, win_recv, grad_send, grad_recv,
):
    scan = lax.axis_index("scan")
    me = lax.axis_index("depth")
    shift = 3 * lax.rem(scan, 2)
    slot = lax.div(me + 4 - shift, STRIDE) - 1
    active = lax.rem(me + 4 - shift, STRIDE) == 0

    def home(i):
        return STRIDE * i + shift

    barrier = pltpu.get_barrier_semaphore()

    @pl.when(active)
    def _():
        def greet(d, carry):
            @pl.when(d != me)
            def _():
                pl.semaphore_signal(barrier, inc=1, device_id=(scan, d), device_id_type=MESH)
            return carry
        lax.fori_loop(0, sections, greet, 0)
        pl.semaphore_wait(barrier, sections - 1)

    @pl.when(jnp.logical_not(active))
    def _():
        def greet(i, carry):
            pl.semaphore_signal(barrier, inc=1, device_id=(scan, home(i)), device_id_type=MESH)
            return carry
        lax.fori_loop(0, num_pos, greet, 0)
        pl.semaphore_wait(barrier, num_pos)

    def window_copy(i):
        return pltpu.make_async_remote_copy(
            src_ref=tw_ref.at[i], dst_ref=trans.at[me], send_sem=win_send.at[i], recv_sem=win_recv.at[me],
            device_id=(scan, home(i)), device_id_type=MESH)

    def send_window(i, carry):
        @pl.when(home(i) != me)
        def _():
            window_copy(i).start()

        @pl.when(home(i) == me)
        def _():
            pltpu.make_async_copy(tw_ref.at[i], trans.at[me], win_recv.at[me]).start()
        return carry

    lax.fori_loop(0, num_pos, send_window, 0)

    def grad_copy(k):
        return pltpu.make_async_remote_copy(
            src_ref=exits.at[k], dst_ref=got_ref.at[slot], send_sem=grad_send.at[k], recv_sem=grad_recv.at[slot],
            device_id=(scan, k), device_id_type=MESH)

    @pl.when(active)
    def _():
        wave[...] = probe_ref[...]

        def step_in(k):
            pltpu.make_async_copy(tw_ref.at[0], trans.at[k], win_recv.at[k]).wait()
            tr, ti = trans[k, 0], trans[k, 1]
            wr, wi = wave[0], wave[1]
            er = wr * tr - wi * ti
            ei = wr * ti + wi * tr
            exits[k, 0] = er
            exits[k, 1] = ei
            return er, ei

        def forward(k, carry):
            er, ei = step_in(k)
            wr, wi = sandwich(er, ei, tab_ref, 0, 2)
            wave[0] = wr
            wave[1] = wi
            return carry

        lax.fori_loop(0, sections - 1, forward, 0)
        er, ei = step_in(sections - 1)
        fr, fi = sandwich(er, ei, tab_ref, 4, 6)
        resid = fr * fr + fi * fi - meas_ref[slot]
        lr, li = sandwich(resid * fr, resid * fi, tab_ref, 6, 4)
        wave[0] = lr
        wave[1] = li

        def grads(k):
            er, ei = exits[k, 0], exits[k, 1]
            lr, li = wave[0], wave[1]
            exits[k, 0] = er * li - ei * lr
            exits[k, 1] = -(er * lr + ei * li)

            @pl.when(k != me)
            def _():
                grad_copy(k).start()

            @pl.when(k == me)
            def _():
                pltpu.make_async_copy(exits.at[k], got_ref.at[slot], grad_recv.at[slot]).start()
            return lr, li

        def backward(j, carry):
            k = sections - 1 - j
            lr, li = grads(k)
            tr, ti = trans[k, 0], trans[k, 1]
            wr, wi = sandwich(tr * lr + ti * li, tr * li - ti * lr, tab_ref, 2, 0)
            wave[0] = wr
            wave[1] = wi
            return carry

        lax.fori_loop(0, sections - 1, backward, 0)
        grads(0)

    def finish(i, carry):
        @pl.when(home(i) != me)
        def _():
            window_copy(i).wait_send()
        pltpu.make_async_copy(tw_ref.at[0], got_ref.at[i], grad_recv.at[i]).wait()
        return carry

    lax.fori_loop(0, num_pos, finish, 0)

    @pl.when(active)
    def _():
        def drain(k, carry):
            @pl.when(k != me)
            def _():
                grad_copy(k).wait_send()
            return carry
        lax.fori_loop(0, sections, drain, 0)


def sum_kernel(parts_ref, phase_ref, absorb_ref, got, own_sem, send_sem, recv_sem):
    me = lax.axis_index("scan")
    depth = lax.axis_index("depth")
    groups, rows = got.shape[0], got.shape[2]
    barrier = pltpu.get_barrier_semaphore()

    def peer(step):
        return lax.rem(me + step, groups)

    def greet(step, carry):
        pl.semaphore_signal(barrier, inc=1, device_id=(peer(step), depth), device_id_type=MESH)
        return carry

    lax.fori_loop(1, groups, greet, 0)
    own = pltpu.make_async_copy(parts_ref.at[:, pl.ds(me * rows, rows), :], got.at[me], own_sem)
    own.start()
    pl.semaphore_wait(barrier, groups - 1)

    def strip(step):
        to = peer(step)
        return pltpu.make_async_remote_copy(
            src_ref=parts_ref.at[:, pl.ds(to * rows, rows), :], dst_ref=got.at[me],
            send_sem=send_sem.at[step], recv_sem=recv_sem.at[me],
            device_id=(to, depth), device_id_type=MESH)

    def send(step, carry):
        strip(step).start()
        return carry

    lax.fori_loop(1, groups, send, 0)
    own.wait()

    def arrive(step, carry):
        one = peer(step)
        pltpu.make_async_copy(got.at[one], got.at[one], recv_sem.at[one]).wait()
        return carry

    lax.fori_loop(1, groups, arrive, 0)
    total = got[0]
    for i in range(1, groups):
        total = total + got[i]
    phase_ref[0] = total[0]
    absorb_ref[0] = total[1]

    def drain(step, carry):
        strip(step).wait_send()
        return carry

    lax.fori_loop(1, groups, drain, 0)


def shards(tab, phase, absorb, probe, offsets, measured):
    win = probe.shape[-1]
    obj = phase.shape[-1]
    num_pos = offsets.shape[0]
    sections = lax.axis_size("depth")
    vmem = pl.BlockSpec(memory_space=pltpu.VMEM)
    smem = pl.BlockSpec(memory_space=pltpu.SMEM)
    limit = 48 * 1024 * 1024
    windows = pl.pallas_call(
        window_kernel,
        out_shape=jax.ShapeDtypeStruct((num_pos, 2, win, win), F32),
        in_specs=[smem, vmem, vmem],
        out_specs=vmem,
        scratch_shapes=[pltpu.VMEM((2, obj + 8, obj), F32)],
        compiler_params=pltpu.CompilerParams(vmem_limit_bytes=limit),
    )(offsets, phase, absorb)
    got = pl.pallas_call(
        functools.partial(chain_kernel, sections, num_pos),
        out_shape=jax.ShapeDtypeStruct((num_pos, 2, win, win), F32),
        in_specs=[vmem] * 4,
        out_specs=vmem,
        scratch_shapes=[
            pltpu.VMEM((sections, 2, win, win), F32),
            pltpu.VMEM((sections, 2, win, win), F32),
            pltpu.VMEM((2, win, win), F32),
            pltpu.SemaphoreType.DMA((num_pos,)),
            pltpu.SemaphoreType.DMA((sections,)),
            pltpu.SemaphoreType.DMA((sections,)),
            pltpu.SemaphoreType.DMA((num_pos,)),
        ],
        compiler_params=pltpu.CompilerParams(
            collective_id=0, has_side_effects=True, vmem_limit_bytes=limit),
    )(windows, probe, measured, tab)
    fields = pl.pallas_call(
        field_kernel,
        out_shape=jax.ShapeDtypeStruct((2, obj, obj), F32),
        in_specs=[smem, vmem],
        out_specs=vmem,
        scratch_shapes=[pltpu.VMEM((2, obj + 8, obj), F32)],
        compiler_params=pltpu.CompilerParams(vmem_limit_bytes=limit),
    )(offsets, got)
    groups = lax.axis_size("scan")
    rows = obj // groups
    return pl.pallas_call(
        sum_kernel,
        out_shape=[jax.ShapeDtypeStruct((1, rows, obj), F32)] * 2,
        in_specs=[vmem],
        out_specs=[vmem, vmem],
        scratch_shapes=[
            pltpu.VMEM((groups, 2, rows, obj), F32),
            pltpu.SemaphoreType.DMA,
            pltpu.SemaphoreType.DMA((groups,)),
            pltpu.SemaphoreType.DMA((groups,)),
        ],
        compiler_params=pltpu.CompilerParams(
            collective_id=1, has_side_effects=True, vmem_limit_bytes=limit),
    )(fields)


def solution(mesh):
    tab = tables(128)
    in_specs = (
        P("depth", None, None),
        P("depth", None, None),
        P(),
        P("scan", None),
        P("scan", None, None),
    )
    out_specs = (P("depth", "scan", None), P("depth", "scan", None))

    def run(phase, absorb, probe, offsets, measured):
        body = functools.partial(shards, jnp.asarray(tab))
        return jax.shard_map(body, mesh=mesh, in_specs=in_specs, out_specs=out_specs, check_vma=False)(
            phase, absorb, probe, offsets, measured)

    return run
```

```python
import functools

import jax
import jax.numpy as jnp
import ml_dtypes
import numpy as np
from jax import lax
from jax.experimental import pallas as pl
from jax.experimental.pallas import tpu as pltpu
from jax.sharding import PartitionSpec as P

MESH = pl.DeviceIdType.MESH
BF16 = jnp.bfloat16
F32 = jnp.float32
LANES = 2
SIDE = 4
AHEAD = 12


def tables(win):
    idx = np.arange(win)
    ang = 2.0 * np.pi * (np.outer(idx, idx) % win) / win
    fwd = np.exp(-1j * ang) / np.sqrt(win)
    signed = np.where(idx < win // 2, idx, idx - win).astype(np.float64)
    chirp = np.exp(-1j * signed**2 / win)
    prop = np.conj(fwd) @ (chirp[:, None] * fwd)
    prop = 0.5 * (prop + prop.T)
    out = []
    for mat in (prop, fwd):
        right = np.block([[mat.real, mat.imag], [-mat.imag, mat.real]])
        left = np.block([[mat.real, -mat.imag], [mat.imag, mat.real]])
        for block in (right, left):
            block = block.astype(np.float32)
            high = block.astype(ml_dtypes.bfloat16)
            low = (block - high.astype(np.float32)).astype(ml_dtypes.bfloat16)
            out += [high, low]
    return np.stack(out)


def split(values):
    high = values.astype(BF16)
    low = (values - high.astype(F32)).astype(BF16)
    return high, low


def sandwich(re, im, tab, right, left):
    win = re.shape[0]
    high, low = split(jnp.concatenate([re, im], axis=1))
    both = jnp.concatenate([high, low], axis=0)
    main = jnp.dot(both, tab[right], preferred_element_type=F32)
    half = main[:win] + main[win:] + jnp.dot(high, tab[right + 1], preferred_element_type=F32)
    high, low = split(jnp.concatenate([half[:, :win], half[:, win:]], axis=0))
    both = jnp.concatenate([high, low], axis=1)
    main = jnp.dot(tab[left], both, preferred_element_type=F32)
    done = main[:, :win] + main[:, win:] + jnp.dot(tab[left + 1], high, preferred_element_type=F32)
    return done[:win], done[win:]


def turned(index):
    first, last = lax.div(index, 8), lax.rem(index, 2)
    return index + 7 * (last - first)


def place():
    depth = lax.axis_index("depth")
    return lax.axis_index("scan"), lax.div(depth, LANES), lax.rem(depth, LANES)


def home(j, z):
    scan = 2 * j + lax.rem(z, 2)
    return scan, LANES * z + lax.rem(lax.div(scan, SIDE), 2)


def corner(off_ref, j):
    z = lax.div(lax.axis_index("depth"), LANES)
    scan = 2 * j + lax.rem(z, 2)
    return off_ref[scan, 0], off_ref[scan, 1]


def around(scan, z, lane, planes, distance):
    return scan, LANES * lax.rem(z + planes + distance, planes) + lane


def strip_rows(z, rows):
    return pl.ds(pl.multiple_of(turned(z) * rows, 8), rows)


def gather_kernel(
    off_ref, phase_ref, absorb_ref, field_ref, corner_ref,
    raw, made, line, raw_sem, turn_sem, line_send, line_recv, send_sem, recv_sem,
):
    scan, z, lane = place()
    groups = lax.axis_size("scan")
    planes = lax.axis_size("depth") // LANES
    rows = made.shape[1]
    rounds = planes // 4
    loads = []
    for part, ref in enumerate((phase_ref, absorb_ref)):
        src = ref.at[0, pl.ds(pl.multiple_of(scan * rows, 8), rows), :]
        loads.append(pltpu.make_async_copy(src, raw.at[part], raw_sem.at[part]))
        loads[-1].start()
    to = (turned(z), LANES * turned(scan) + lane)
    stays = turned(z) == scan
    near = (-2, -1, 1, 2)

    barrier = pltpu.get_barrier_semaphore()
    for distance in near:
        pl.semaphore_signal(
            barrier, inc=1, device_id=around(scan, z, lane, planes, distance), device_id_type=MESH)

    @pl.when(jnp.logical_not(stays))
    def _():
        pl.semaphore_signal(barrier, inc=1, device_id=to, device_id_type=MESH)

    def greet(step, carry):
        other = (lax.rem(scan + step, groups), LANES * z + lane)
        pl.semaphore_signal(barrier, inc=1, device_id=other, device_id_type=MESH)
        return carry

    lax.fori_loop(1, groups, greet, 0)
    line[...] = jnp.zeros_like(line)
    line[:, : off_ref.shape[1]] = off_ref[...]
    for load in loads:
        load.wait()
    amp = jnp.exp(-raw[1])
    made[0] = amp * jnp.cos(raw[0])
    made[1] = amp * jnp.sin(raw[0])

    turn = pltpu.make_async_remote_copy(
        src_ref=made, dst_ref=field_ref.at[:, strip_rows(turned(scan), rows), :],
        send_sem=turn_sem.at[0], recv_sem=turn_sem.at[1], device_id=to, device_id_type=MESH)
    stay = pltpu.make_async_copy(made, field_ref.at[:, strip_rows(z, rows), :], turn_sem.at[1])

    @pl.when(stays)
    def _():
        pl.semaphore_wait(barrier, len(near) + groups - 1)
        stay.start()

    @pl.when(jnp.logical_not(stays))
    def _():
        pl.semaphore_wait(barrier, len(near) + groups)
        turn.start()

    own_line = line.at[pl.ds(lax.div(z, 2), 1), :]
    own = pltpu.make_async_copy(own_line, corner_ref.at[pl.ds(scan, 1), :], line_recv.at[scan])
    own.start()

    def tell(step):
        return pltpu.make_async_remote_copy(
            src_ref=own_line, dst_ref=corner_ref.at[pl.ds(scan, 1), :],
            send_sem=line_send.at[step], recv_sem=line_recv.at[scan],
            device_id=(lax.rem(scan + step, groups), LANES * z + lane), device_id_type=MESH)

    def start_tell(step, carry):
        tell(step).start()
        return carry

    lax.fori_loop(1, groups, start_tell, 0)
    stay.wait()

    def passing(step, way, distance):
        sign = 1 if way == 0 else -1
        whose = lax.rem(z + planes - sign * 2 * step, planes)
        block = field_ref.at[:, strip_rows(whose, rows), :]
        return pltpu.make_async_remote_copy(
            src_ref=block, dst_ref=block,
            send_sem=send_sem.at[way, step, distance - 1], recv_sem=recv_sem.at[way, step, distance - 1],
            device_id=around(scan, z, lane, planes, sign * distance), device_id_type=MESH)

    def goes(step, way, distance):
        return not (way == 1 and step == rounds - 1 and distance == 2)

    plan = [(step, way, distance) for step in range(rounds) for distance in (2, 1) for way in range(2)
            if goes(step, way, distance)]
    for step, way, distance in plan:
        if step > 0 and (distance == 2 or not goes(step, way, 2)):
            passing(step - 1, way, 2).wait_recv()
        passing(step, way, distance).start()
    passing(rounds - 1, 0, 2).wait_recv()
    for step, way, distance in plan:
        if distance == 1:
            passing(step, way, distance).wait_recv()
    for step, way, distance in plan:
        passing(step, way, distance).wait_send()

    @pl.when(jnp.logical_not(stays))
    def _():
        turn.wait_send()

    def end_tell(step, carry):
        one = lax.rem(scan + step, groups)
        pltpu.make_async_copy(own_line, corner_ref.at[pl.ds(one, 1), :], line_recv.at[one]).wait()

        @pl.when(step > 0)
        def _():
            tell(step).wait_send()
        return carry

    lax.fori_loop(0, groups, end_tell, 0)


def window_kernel(off_ref, field_ref, out_ref, field):
    win = out_ref.shape[-1]
    obj = field_ref.shape[-1]
    field[:, :obj] = field_ref[...]

    def one(j, carry):
        row, col = corner(off_ref, j)
        high = lax.div(row, 8)
        low = row - 8 * high
        for part in range(2):
            rows = field[part, pl.ds(pl.multiple_of(8 * high, 8), win + 8), :]
            cols = pltpu.roll(rows, lax.rem(obj - col, obj), 1)[:, :win]
            out_ref[j, part] = pltpu.roll(cols, lax.rem(win + 8 - low, win + 8), 0)[:win]
        return carry

    lax.fori_loop(0, out_ref.shape[0], one, 0)


def field_kernel(off_ref, got_ref, out_ref, field):
    win = got_ref.shape[-1]
    obj = out_ref.shape[-1]
    field[...] = jnp.zeros_like(field)

    def one(j, carry):
        row, col = corner(off_ref, j)
        high = lax.div(row, 8)
        low = row - 8 * high
        for part in range(2):
            tall = jnp.concatenate([got_ref[j, part], jnp.zeros((8, win), F32)], axis=0)
            tall = pltpu.roll(tall, low, 0)
            wide = jnp.concatenate([tall, jnp.zeros((win + 8, obj - win), F32)], axis=1)
            field[part, pl.ds(pl.multiple_of(8 * high, 8), win + 8), :] += pltpu.roll(wide, col, 1)
        return carry

    lax.fori_loop(0, got_ref.shape[0], one, 0)
    out_ref[...] = field[:, :obj]


def chain_kernel(
    sections, num_pos, tw_ref, probe_ref, meas_ref, tab_ref, got_ref,
    trans, exits, wave, go_sem, win_send, win_recv, grad_send, grad_recv,
):
    scan, z, lane = place()
    depth = LANES * z + lane
    mine = 2 * turned(scan) + lane
    slot = lax.div(z, 2)
    member = lax.div(scan, 2)

    def is_home(on_scan, on_lane):
        return jnp.logical_and(lax.rem(on_scan, 2) == lax.rem(z, 2), on_lane == lax.rem(lax.div(on_scan, SIDE), 2))

    active = is_home(scan, lane)

    def owner(k):
        return turned(lax.div(k, LANES)), LANES * z + lax.rem(k, LANES)

    barrier = pltpu.get_barrier_semaphore()

    @pl.when(active)
    def _():
        def greet(k, carry):
            @pl.when(k != mine)
            def _():
                pl.semaphore_signal(barrier, inc=1, device_id=owner(k), device_id_type=MESH)
            return carry
        lax.fori_loop(0, sections, greet, 0)
        pl.semaphore_wait(barrier, sections - 1)

    @pl.when(jnp.logical_not(active))
    def _():
        def greet(j, carry):
            pl.semaphore_signal(barrier, inc=1, device_id=home(j, z), device_id_type=MESH)
            return carry
        lax.fori_loop(0, num_pos, greet, 0)
        pl.semaphore_wait(barrier, num_pos)

    def is_here(j):
        return jnp.logical_and(active, j == member)

    def window_copy(j):
        return pltpu.make_async_remote_copy(
            src_ref=tw_ref.at[j], dst_ref=trans.at[mine], send_sem=win_send.at[j], recv_sem=win_recv.at[mine],
            device_id=home(j, z), device_id_type=MESH)

    def send_window(step, carry):
        j = lax.rem(step + member, num_pos)
        here = is_here(j)

        @pl.when(jnp.logical_not(here))
        def _():
            window_copy(j).start()

        @pl.when(here)
        def _():
            pltpu.make_async_copy(tw_ref.at[j], trans.at[mine], win_recv.at[mine]).start()
        return carry

    def send_windows():
        lax.fori_loop(0, num_pos, send_window, 0)

    @pl.when(mine < AHEAD)
    def _():
        send_windows()

    @pl.when(jnp.logical_and(jnp.logical_not(active), mine >= AHEAD))
    def _():
        pl.semaphore_wait(go_sem, 1)
        send_windows()

    def call_up(k):
        @pl.when(jnp.logical_and(k == mine, k >= AHEAD))
        def _():
            send_windows()

        to, on_plane = owner(k)
        on_lane = on_plane - LANES * z
        awaits = jnp.logical_not(is_home(to, on_lane))
        chosen = jnp.logical_and(lax.rem(k, num_pos) == member, k < sections)

        @pl.when(jnp.logical_and(awaits, chosen))
        def _():
            pl.semaphore_signal(go_sem, inc=1, device_id=owner(k), device_id_type=MESH)

    def grad_copy(k):
        return pltpu.make_async_remote_copy(
            src_ref=exits.at[k], dst_ref=got_ref.at[member], send_sem=grad_send.at[k],
            recv_sem=grad_recv.at[member], device_id=owner(k), device_id_type=MESH)

    @pl.when(active)
    def _():
        wave[...] = probe_ref[...]

        def step_in(k):
            pltpu.make_async_copy(tw_ref.at[0], trans.at[k], win_recv.at[k]).wait()
            tr, ti = trans[k, 0], trans[k, 1]
            wr, wi = wave[0], wave[1]
            er = wr * tr - wi * ti
            ei = wr * ti + wi * tr
            exits[k, 0] = er
            exits[k, 1] = ei
            return er, ei

        def forward(k, carry):
            call_up(k + AHEAD)
            er, ei = step_in(k)
            wr, wi = sandwich(er, ei, tab_ref, 0, 2)
            wave[0] = wr
            wave[1] = wi
            return carry

        lax.fori_loop(0, sections - 1, forward, 0)
        er, ei = step_in(sections - 1)
        fr, fi = sandwich(er, ei, tab_ref, 4, 6)
        resid = fr * fr + fi * fi - meas_ref[slot]
        lr, li = sandwich(resid * fr, resid * fi, tab_ref, 6, 4)
        wave[0] = lr
        wave[1] = li

        def grads(k):
            er, ei = exits[k, 0], exits[k, 1]
            lr, li = wave[0], wave[1]
            exits[k, 0] = er * li - ei * lr
            exits[k, 1] = -(er * lr + ei * li)

            @pl.when(k != mine)
            def _():
                grad_copy(k).start()

            @pl.when(k == mine)
            def _():
                pltpu.make_async_copy(exits.at[k], got_ref.at[member], grad_recv.at[member]).start()
            return lr, li

        def backward(j, carry):
            k = sections - 1 - j
            lr, li = grads(k)
            tr, ti = trans[k, 0], trans[k, 1]
            wr, wi = sandwich(tr * lr + ti * li, tr * li - ti * lr, tab_ref, 2, 0)
            wave[0] = wr
            wave[1] = wi
            return carry

        lax.fori_loop(0, sections - 1, backward, 0)
        grads(0)

    def finish(j, carry):
        @pl.when(jnp.logical_not(is_here(j)))
        def _():
            window_copy(j).wait_send()
        pltpu.make_async_copy(tw_ref.at[0], got_ref.at[j], grad_recv.at[j]).wait()
        return carry

    lax.fori_loop(0, num_pos, finish, 0)

    @pl.when(active)
    def _():
        def drain(k, carry):
            @pl.when(k != mine)
            def _():
                grad_copy(k).wait_send()
            return carry
        lax.fori_loop(0, sections, drain, 0)


def sum_kernel(parts_ref, phase_ref, absorb_ref, got, made, last, turn_sem, send_sem, recv_sem):
    scan, z, lane = place()
    planes = lax.axis_size("depth") // LANES
    rows = last.shape[2]
    rounds = planes // 4
    to = (turned(z), LANES * turned(scan) + lane)
    stays = turned(z) == scan
    near = (-2, -1, 1, 2)
    barrier = pltpu.get_barrier_semaphore()
    for distance in near:
        pl.semaphore_signal(
            barrier, inc=1, device_id=around(scan, z, lane, planes, distance), device_id_type=MESH)

    @pl.when(jnp.logical_not(stays))
    def _():
        pl.semaphore_signal(barrier, inc=1, device_id=to, device_id_type=MESH)
        pl.semaphore_wait(barrier, len(near) + 1)

    @pl.when(stays)
    def _():
        pl.semaphore_wait(barrier, len(near))

    def strip(way, ahead):
        sign = 1 if way == 0 else -1
        return parts_ref.at[:, strip_rows(lax.rem(z + planes + sign * ahead, planes), rows), :]

    def goes(step, way, distance):
        return not (way == 1 and step == 0 and distance == 2)

    def passing(step, way, distance):
        ahead = planes // 2 - 2 * step - (2 - distance)
        bare = distance == 1 or step == 0 or (way == 1 and step == 0)
        return pltpu.make_async_remote_copy(
            src_ref=strip(way, ahead) if bare else made.at[way, step - 1],
            dst_ref=got.at[way, step, distance - 1],
            send_sem=send_sem.at[way, step, distance - 1], recv_sem=recv_sem.at[way, step, distance - 1],
            device_id=around(scan, z, lane, planes, distance if way == 0 else -distance), device_id_type=MESH)

    def arrived(step, way):
        passing(step, way, 1).wait_recv()
        total = got[way, step, 0]
        if goes(step, way, 2):
            passing(step, way, 2).wait_recv()
            total = total + got[way, step, 1]
        return total

    for way in range(2):
        if goes(0, way, 2):
            passing(0, way, 2).start()
    for way in range(2):
        passing(0, way, 1).start()
    for way in range(2):
        passing(1, way, 1).start()
    for step in range(1, rounds):
        for way in range(2):
            ahead = planes // 2 - 2 * step
            made[way, step - 1] = strip(way, ahead)[...] + arrived(step - 1, way)
            passing(step, way, 2).start()
        if step + 1 < rounds:
            for way in range(2):
                passing(step + 1, way, 1).start()
    last[0] = strip(0, 0)[...] + (arrived(rounds - 1, 0) + arrived(rounds - 1, 1))
    turn = pltpu.make_async_remote_copy(
        src_ref=last.at[0], dst_ref=last.at[1], send_sem=turn_sem.at[0], recv_sem=turn_sem.at[1],
        device_id=to, device_id_type=MESH)

    @pl.when(jnp.logical_not(stays))
    def _():
        turn.start()
        turn.wait()

    @pl.when(stays)
    def _():
        last[1] = last[0]

    phase_ref[0] = last[1, 0]
    absorb_ref[0] = last[1, 1]
    for step in range(rounds):
        for way in range(2):
            for distance in (1, 2):
                if goes(step, way, distance):
                    passing(step, way, distance).wait_send()


def shards(tab, phase, absorb, probe, offsets, measured):
    win = probe.shape[-1]
    obj = phase.shape[-1]
    num_pos = offsets.shape[0]
    sections = lax.axis_size("depth")
    vmem = pl.BlockSpec(memory_space=pltpu.VMEM)
    smem = pl.BlockSpec(memory_space=pltpu.SMEM)
    anywhere = pl.BlockSpec(memory_space=pl.ANY)
    limit = 48 * 1024 * 1024
    groups = lax.axis_size("scan")
    rows = obj // groups
    rounds = sections // LANES // 4
    field, corners = pl.pallas_call(
        gather_kernel,
        out_shape=[
            jax.ShapeDtypeStruct((2, obj, obj), F32),
            jax.ShapeDtypeStruct((groups, 128), jnp.int32),
        ],
        in_specs=[vmem, anywhere, anywhere],
        out_specs=[vmem, vmem],
        scratch_shapes=[
            pltpu.VMEM((2, rows, obj), F32),
            pltpu.VMEM((2, rows, obj), F32),
            pltpu.VMEM((num_pos, 128), jnp.int32),
            pltpu.SemaphoreType.DMA((2,)),
            pltpu.SemaphoreType.DMA((2,)),
            pltpu.SemaphoreType.DMA((groups,)),
            pltpu.SemaphoreType.DMA((groups,)),
            pltpu.SemaphoreType.DMA((2, rounds, 2)),
            pltpu.SemaphoreType.DMA((2, rounds, 2)),
        ],
        compiler_params=pltpu.CompilerParams(
            collective_id=2, has_side_effects=True, vmem_limit_bytes=60 * 1024 * 1024),
    )(offsets, phase, absorb)
    windows = pl.pallas_call(
        window_kernel,
        out_shape=jax.ShapeDtypeStruct((num_pos, 2, win, win), F32),
        in_specs=[smem, vmem],
        out_specs=vmem,
        scratch_shapes=[pltpu.VMEM((2, obj + 8, obj), F32)],
        compiler_params=pltpu.CompilerParams(vmem_limit_bytes=limit),
    )(corners, field)
    got = pl.pallas_call(
        functools.partial(chain_kernel, sections, num_pos),
        out_shape=jax.ShapeDtypeStruct((num_pos, 2, win, win), F32),
        in_specs=[vmem] * 4,
        out_specs=vmem,
        scratch_shapes=[
            pltpu.VMEM((sections, 2, win, win), F32),
            pltpu.VMEM((sections, 2, win, win), F32),
            pltpu.VMEM((2, win, win), F32),
            pltpu.SemaphoreType.REGULAR,
            pltpu.SemaphoreType.DMA((num_pos,)),
            pltpu.SemaphoreType.DMA((sections,)),
            pltpu.SemaphoreType.DMA((sections,)),
            pltpu.SemaphoreType.DMA((num_pos,)),
        ],
        compiler_params=pltpu.CompilerParams(
            collective_id=0, has_side_effects=True, vmem_limit_bytes=limit),
    )(windows, probe, measured, tab)
    fields = pl.pallas_call(
        field_kernel,
        out_shape=jax.ShapeDtypeStruct((2, obj, obj), F32),
        in_specs=[smem, vmem],
        out_specs=vmem,
        scratch_shapes=[pltpu.VMEM((2, obj + 8, obj), F32)],
        compiler_params=pltpu.CompilerParams(vmem_limit_bytes=limit),
    )(corners, got)
    return pl.pallas_call(
        sum_kernel,
        out_shape=[jax.ShapeDtypeStruct((1, rows, obj), F32)] * 2,
        in_specs=[vmem],
        out_specs=[vmem, vmem],
        scratch_shapes=[
            pltpu.VMEM((2, rounds, 2, 2, rows, obj), F32),
            pltpu.VMEM((2, rounds - 1, 2, rows, obj), F32),
            pltpu.VMEM((2, 2, rows, obj), F32),
            pltpu.SemaphoreType.DMA((2,)),
            pltpu.SemaphoreType.DMA((2, rounds, 2)),
            pltpu.SemaphoreType.DMA((2, rounds, 2)),
        ],
        compiler_params=pltpu.CompilerParams(
            collective_id=1, has_side_effects=True, vmem_limit_bytes=limit),
    )(fields)


def solution(mesh):
    tab = tables(128)
    in_specs = (
        P("depth", None, None),
        P("depth", None, None),
        P(),
        P("scan", None),
        P("scan", None, None),
    )
    out_specs = (P("depth", "scan", None), P("depth", "scan", None))

    def run(phase, absorb, probe, offsets, measured):
        body = functools.partial(shards, jnp.asarray(tab))
        return jax.shard_map(body, mesh=mesh, in_specs=in_specs, out_specs=out_specs, check_vma=False)(
            phase, absorb, probe, offsets, measured)

    return run
```

```python
import functools

import jax
import jax.numpy as jnp
import ml_dtypes
import numpy as np
from jax import lax
from jax.experimental import pallas as pl
from jax.experimental.pallas import tpu as pltpu
from jax.sharding import PartitionSpec as P

MESH = pl.DeviceIdType.MESH
BF16 = jnp.bfloat16
F32 = jnp.float32
LANES = 2
SIDE = 4
AHEAD = 14


def tables(win):
    idx = np.arange(win)
    ang = 2.0 * np.pi * (np.outer(idx, idx) % win) / win
    fwd = np.exp(-1j * ang) / np.sqrt(win)
    signed = np.where(idx < win // 2, idx, idx - win).astype(np.float64)
    chirp = np.exp(-1j * signed**2 / win)
    prop = np.conj(fwd) @ (chirp[:, None] * fwd)
    prop = 0.5 * (prop + prop.T)
    out = []
    for mat in (prop, fwd):
        right = np.block([[mat.real, mat.imag], [-mat.imag, mat.real]])
        left = np.block([[mat.real, -mat.imag], [mat.imag, mat.real]])
        for block in (right, left):
            block = block.astype(np.float32)
            high = block.astype(ml_dtypes.bfloat16)
            low = (block - high.astype(np.float32)).astype(ml_dtypes.bfloat16)
            out += [high, low]
    return np.stack(out)


def split(values):
    high = values.astype(BF16)
    low = (values - high.astype(F32)).astype(BF16)
    return high, low


def sandwich(re, im, tab, right, left):
    win = re.shape[0]
    high, low = split(jnp.concatenate([re, im], axis=1))
    both = jnp.concatenate([high, low], axis=0)
    main = jnp.dot(both, tab[right], preferred_element_type=F32)
    half = main[:win] + main[win:] + jnp.dot(high, tab[right + 1], preferred_element_type=F32)
    high, low = split(jnp.concatenate([half[:, :win], half[:, win:]], axis=0))
    both = jnp.concatenate([high, low], axis=1)
    main = jnp.dot(tab[left], both, preferred_element_type=F32)
    done = main[:, :win] + main[:, win:] + jnp.dot(tab[left + 1], high, preferred_element_type=F32)
    return done[:win], done[win:]


def turned(index):
    first, last = lax.div(index, 8), lax.rem(index, 2)
    return index + 7 * (last - first)


def place():
    depth = lax.axis_index("depth")
    return lax.axis_index("scan"), lax.div(depth, LANES), lax.rem(depth, LANES)


def home(j, z):
    scan = 2 * j + lax.rem(z, 2)
    return scan, LANES * z + lax.rem(lax.div(scan, SIDE), 2)


def corner(off_ref, j):
    z = lax.div(lax.axis_index("depth"), LANES)
    scan = 2 * j + lax.rem(z, 2)
    return off_ref[scan, 0], off_ref[scan, 1]


def around(scan, z, lane, planes, distance):
    return scan, LANES * lax.rem(z + planes + distance, planes) + lane


def strip_rows(z, rows):
    return pl.ds(pl.multiple_of(turned(z) * rows, 8), rows)


def gather_kernel(
    off_ref, raw, field_ref, corner_ref,
    near_off, made, line, off_sem, turn_sem, line_send, line_recv, send_sem, recv_sem,
):
    scan, z, lane = place()
    groups = lax.axis_size("scan")
    planes = lax.axis_size("depth") // LANES
    rows = made.shape[1]
    rounds = planes // 4
    fetch = pltpu.make_async_copy(off_ref, near_off, off_sem)
    fetch.start()
    to = (turned(z), LANES * turned(scan) + lane)
    stays = turned(z) == scan
    near = (-2, -1, 1, 2)

    barrier = pltpu.get_barrier_semaphore()
    for distance in near:
        pl.semaphore_signal(
            barrier, inc=1, device_id=around(scan, z, lane, planes, distance), device_id_type=MESH)

    @pl.when(jnp.logical_not(stays))
    def _():
        pl.semaphore_signal(barrier, inc=1, device_id=to, device_id_type=MESH)

    def greet(step, carry):
        other = (lax.rem(scan + step, groups), LANES * z + lane)
        pl.semaphore_signal(barrier, inc=1, device_id=other, device_id_type=MESH)
        return carry

    lax.fori_loop(1, groups, greet, 0)
    line[...] = jnp.zeros_like(line)
    field_ref[:, groups * rows :] = jnp.zeros((2, field_ref.shape[1] - groups * rows, field_ref.shape[2]), F32)
    fetch.wait()
    line[:, : near_off.shape[1]] = near_off[...]
    amp = jnp.exp(-raw[1])
    made[0] = amp * jnp.cos(raw[0])
    made[1] = amp * jnp.sin(raw[0])

    turn = pltpu.make_async_remote_copy(
        src_ref=made, dst_ref=field_ref.at[:, strip_rows(turned(scan), rows), :],
        send_sem=turn_sem.at[0], recv_sem=turn_sem.at[1], device_id=to, device_id_type=MESH)
    stay = pltpu.make_async_copy(made, field_ref.at[:, strip_rows(z, rows), :], turn_sem.at[1])

    @pl.when(stays)
    def _():
        pl.semaphore_wait(barrier, len(near) + groups - 1)
        stay.start()

    @pl.when(jnp.logical_not(stays))
    def _():
        pl.semaphore_wait(barrier, len(near) + groups)
        turn.start()

    own_line = line.at[pl.ds(lax.div(z, 2), 1), :]
    own = pltpu.make_async_copy(own_line, corner_ref.at[pl.ds(scan, 1), :], line_recv.at[scan])
    own.start()

    def tell(step):
        return pltpu.make_async_remote_copy(
            src_ref=own_line, dst_ref=corner_ref.at[pl.ds(scan, 1), :],
            send_sem=line_send.at[step], recv_sem=line_recv.at[scan],
            device_id=(lax.rem(scan + step, groups), LANES * z + lane), device_id_type=MESH)

    def start_tell(step, carry):
        tell(step).start()
        return carry

    lax.fori_loop(1, groups, start_tell, 0)
    stay.wait()

    def passing(step, way, distance):
        sign = 1 if way == 0 else -1
        whose = lax.rem(z + planes - sign * 2 * step, planes)
        block = field_ref.at[:, strip_rows(whose, rows), :]
        return pltpu.make_async_remote_copy(
            src_ref=block, dst_ref=block,
            send_sem=send_sem.at[way, step, distance - 1], recv_sem=recv_sem.at[way, step, distance - 1],
            device_id=around(scan, z, lane, planes, sign * distance), device_id_type=MESH)

    def goes(step, way, distance):
        return not (way == 1 and step == rounds - 1 and distance == 2)

    plan = [(step, way, distance) for step in range(rounds) for distance in (2, 1) for way in range(2)
            if goes(step, way, distance)]
    for step, way, distance in plan:
        if step > 0 and (distance == 2 or not goes(step, way, 2)):
            passing(step - 1, way, 2).wait_recv()
        passing(step, way, distance).start()
    passing(rounds - 1, 0, 2).wait_recv()
    for step, way, distance in plan:
        if distance == 1:
            passing(step, way, distance).wait_recv()
    for step, way, distance in plan:
        passing(step, way, distance).wait_send()

    @pl.when(jnp.logical_not(stays))
    def _():
        turn.wait_send()

    def end_tell(step, carry):
        one = lax.rem(scan + step, groups)
        pltpu.make_async_copy(own_line, corner_ref.at[pl.ds(one, 1), :], line_recv.at[one]).wait()

        @pl.when(step > 0)
        def _():
            tell(step).wait_send()
        return carry

    lax.fori_loop(0, groups, end_tell, 0)


def window_kernel(corner_ref, field_ref, out_ref, off_ref, off_sem):
    win = out_ref.shape[-1]
    obj = field_ref.shape[-1]
    fetch = pltpu.make_async_copy(corner_ref, off_ref, off_sem)
    fetch.start()
    fetch.wait()

    def one(j, carry):
        row, col = corner(off_ref, j)
        high = lax.div(row, 8)
        low = row - 8 * high
        for part in range(2):
            rows = field_ref[part, pl.ds(pl.multiple_of(8 * high, 8), win + 8), :]
            cols = pltpu.roll(rows, lax.rem(obj - col, obj), 1)[:, :win]
            out_ref[j, part] = pltpu.roll(cols, lax.rem(win + 8 - low, win + 8), 0)[:win]
        return carry

    lax.fori_loop(0, out_ref.shape[0], one, 0)


def field_kernel(corner_ref, got_ref, out_ref, off_ref, off_sem):
    win = got_ref.shape[-1]
    obj = out_ref.shape[-1]
    fetch = pltpu.make_async_copy(corner_ref, off_ref, off_sem)
    fetch.start()
    out_ref[...] = jnp.zeros_like(out_ref)
    fetch.wait()

    def one(j, carry):
        row, col = corner(off_ref, j)
        high = lax.div(row, 8)
        low = row - 8 * high
        for part in range(2):
            tall = jnp.concatenate([got_ref[j, part], jnp.zeros((8, win), F32)], axis=0)
            tall = pltpu.roll(tall, low, 0)
            wide = jnp.concatenate([tall, jnp.zeros((win + 8, obj - win), F32)], axis=1)
            out_ref[part, pl.ds(pl.multiple_of(8 * high, 8), win + 8), :] += pltpu.roll(wide, col, 1)
        return carry

    lax.fori_loop(0, got_ref.shape[0], one, 0)


def chain_kernel(
    sections, num_pos, tw_ref, probe_ref, all_meas_ref, all_tab_ref, got_ref,
    trans, exits, wave, meas_ref, tab_ref, load_sem, go_sem, win_send, win_recv, grad_send, grad_recv,
):
    scan, z, lane = place()
    depth = LANES * z + lane
    mine = 2 * turned(scan) + lane
    slot = lax.div(z, 2)
    member = lax.div(scan, 2)

    def is_home(on_scan, on_lane):
        return jnp.logical_and(lax.rem(on_scan, 2) == lax.rem(z, 2), on_lane == lax.rem(lax.div(on_scan, SIDE), 2))

    active = is_home(scan, lane)

    def owner(k):
        return turned(lax.div(k, LANES)), LANES * z + lax.rem(k, LANES)

    loads = [
        pltpu.make_async_copy(src, dst, load_sem.at[i])
        for i, (src, dst) in enumerate(
            ((probe_ref, wave), (all_meas_ref.at[slot], meas_ref), (all_tab_ref, tab_ref)))
    ]
    for load in loads:
        load.start()
    barrier = pltpu.get_barrier_semaphore()

    @pl.when(active)
    def _():
        def greet(k, carry):
            @pl.when(k != mine)
            def _():
                pl.semaphore_signal(barrier, inc=1, device_id=owner(k), device_id_type=MESH)
            return carry
        lax.fori_loop(0, sections, greet, 0)

    @pl.when(jnp.logical_not(active))
    def _():
        def greet(j, carry):
            pl.semaphore_signal(barrier, inc=1, device_id=home(j, z), device_id_type=MESH)
            return carry
        lax.fori_loop(0, num_pos, greet, 0)

    @pl.when(active)
    def _():
        pl.semaphore_wait(barrier, sections - 1)

    @pl.when(jnp.logical_not(active))
    def _():
        pl.semaphore_wait(barrier, num_pos)

    def is_here(j):
        return jnp.logical_and(active, j == member)

    def window_copy(j):
        return pltpu.make_async_remote_copy(
            src_ref=tw_ref.at[j], dst_ref=trans.at[mine], send_sem=win_send.at[j], recv_sem=win_recv.at[mine],
            device_id=home(j, z), device_id_type=MESH)

    def send_window(step, carry):
        j = lax.rem(step + member, num_pos)
        here = is_here(j)

        @pl.when(jnp.logical_not(here))
        def _():
            window_copy(j).start()

        @pl.when(here)
        def _():
            pltpu.make_async_copy(tw_ref.at[j], trans.at[mine], win_recv.at[mine]).start()
        return carry

    def send_windows():
        lax.fori_loop(0, num_pos, send_window, 0)

    @pl.when(mine < AHEAD)
    def _():
        send_windows()

    @pl.when(jnp.logical_and(jnp.logical_not(active), mine >= AHEAD))
    def _():
        pl.semaphore_wait(go_sem, 1)
        send_windows()

    def call_up(k):
        @pl.when(jnp.logical_and(k == mine, k >= AHEAD))
        def _():
            send_windows()

        to, on_plane = owner(k)
        on_lane = on_plane - LANES * z
        awaits = jnp.logical_not(is_home(to, on_lane))
        chosen = jnp.logical_and(lax.rem(k, num_pos) == member, k < sections)

        @pl.when(jnp.logical_and(awaits, chosen))
        def _():
            pl.semaphore_signal(go_sem, inc=1, device_id=owner(k), device_id_type=MESH)

    def grad_copy(k):
        return pltpu.make_async_remote_copy(
            src_ref=exits.at[k], dst_ref=got_ref.at[member], send_sem=grad_send.at[k],
            recv_sem=grad_recv.at[member], device_id=owner(k), device_id_type=MESH)

    for load in loads:
        load.wait()

    @pl.when(active)
    def _():
        def step_in(k):
            pltpu.make_async_copy(tw_ref.at[0], trans.at[k], win_recv.at[k]).wait()
            tr, ti = trans[k, 0], trans[k, 1]
            wr, wi = wave[0], wave[1]
            er = wr * tr - wi * ti
            ei = wr * ti + wi * tr
            exits[k, 0] = er
            exits[k, 1] = ei
            return er, ei

        def forward(k, carry):
            call_up(k + AHEAD)
            er, ei = step_in(k)
            wr, wi = sandwich(er, ei, tab_ref, 0, 2)
            wave[0] = wr
            wave[1] = wi
            return carry

        lax.fori_loop(0, sections - 1, forward, 0, unroll=2)
        er, ei = step_in(sections - 1)
        fr, fi = sandwich(er, ei, tab_ref, 4, 6)
        resid = fr * fr + fi * fi - meas_ref[...]
        lr, li = sandwich(resid * fr, resid * fi, tab_ref, 6, 4)
        wave[0] = lr
        wave[1] = li

        def grads(k):
            er, ei = exits[k, 0], exits[k, 1]
            lr, li = wave[0], wave[1]
            exits[k, 0] = er * li - ei * lr
            exits[k, 1] = -(er * lr + ei * li)

            @pl.when(k != mine)
            def _():
                grad_copy(k).start()

            @pl.when(k == mine)
            def _():
                pltpu.make_async_copy(exits.at[k], got_ref.at[member], grad_recv.at[member]).start()
            return lr, li

        def backward(j, carry):
            k = sections - 1 - j
            lr, li = grads(k)
            tr, ti = trans[k, 0], trans[k, 1]
            wr, wi = sandwich(tr * lr + ti * li, tr * li - ti * lr, tab_ref, 2, 0)
            wave[0] = wr
            wave[1] = wi
            return carry

        lax.fori_loop(0, sections - 1, backward, 0, unroll=2)
        grads(0)

    def finish(j, carry):
        @pl.when(jnp.logical_not(is_here(j)))
        def _():
            window_copy(j).wait_send()
        pltpu.make_async_copy(tw_ref.at[0], got_ref.at[j], grad_recv.at[j]).wait()
        return carry

    lax.fori_loop(0, num_pos, finish, 0)

    @pl.when(active)
    def _():
        def drain(k, carry):
            @pl.when(k != mine)
            def _():
                grad_copy(k).wait_send()
            return carry
        lax.fori_loop(0, sections, drain, 0)


def sum_kernel(parts_ref, phase_ref, absorb_ref, got, made, last, turn_sem, send_sem, recv_sem):
    scan, z, lane = place()
    planes = lax.axis_size("depth") // LANES
    rows = last.shape[2]
    rounds = planes // 4
    to = (turned(z), LANES * turned(scan) + lane)
    stays = turned(z) == scan
    near = (-2, -1, 1, 2)
    barrier = pltpu.get_barrier_semaphore()
    for distance in near:
        pl.semaphore_signal(
            barrier, inc=1, device_id=around(scan, z, lane, planes, distance), device_id_type=MESH)

    @pl.when(jnp.logical_not(stays))
    def _():
        pl.semaphore_signal(barrier, inc=1, device_id=to, device_id_type=MESH)
        pl.semaphore_wait(barrier, len(near) + 1)

    @pl.when(stays)
    def _():
        pl.semaphore_wait(barrier, len(near))

    def strip(way, ahead):
        sign = 1 if way == 0 else -1
        return parts_ref.at[:, strip_rows(lax.rem(z + planes + sign * ahead, planes), rows), :]

    def goes(step, way, distance):
        return not (way == 1 and step == 0 and distance == 2)

    def passing(step, way, distance):
        ahead = planes // 2 - 2 * step - (2 - distance)
        bare = distance == 1 or step == 0 or (way == 1 and step == 0)
        return pltpu.make_async_remote_copy(
            src_ref=strip(way, ahead) if bare else made.at[way, step - 1],
            dst_ref=got.at[way, step, distance - 1],
            send_sem=send_sem.at[way, step, distance - 1], recv_sem=recv_sem.at[way, step, distance - 1],
            device_id=around(scan, z, lane, planes, distance if way == 0 else -distance), device_id_type=MESH)

    def arrived(step, way):
        passing(step, way, 1).wait_recv()
        total = got[way, step, 0]
        if goes(step, way, 2):
            passing(step, way, 2).wait_recv()
            total = total + got[way, step, 1]
        return total

    for way in range(2):
        if goes(0, way, 2):
            passing(0, way, 2).start()
    for way in range(2):
        passing(0, way, 1).start()
    for way in range(2):
        passing(1, way, 1).start()
    for step in range(1, rounds):
        for way in range(2):
            ahead = planes // 2 - 2 * step
            made[way, step - 1] = strip(way, ahead)[...] + arrived(step - 1, way)
            passing(step, way, 2).start()
        if step + 1 < rounds:
            for way in range(2):
                passing(step + 1, way, 1).start()
    last[0] = strip(0, 0)[...] + (arrived(rounds - 1, 0) + arrived(rounds - 1, 1))
    turn = pltpu.make_async_remote_copy(
        src_ref=last.at[0], dst_ref=last.at[1], send_sem=turn_sem.at[0], recv_sem=turn_sem.at[1],
        device_id=to, device_id_type=MESH)

    @pl.when(jnp.logical_not(stays))
    def _():
        turn.start()
        turn.wait()

    @pl.when(stays)
    def _():
        last[1] = last[0]

    phase_ref[0] = last[1, 0]
    absorb_ref[0] = last[1, 1]
    for step in range(rounds):
        for way in range(2):
            for distance in (1, 2):
                if goes(step, way, distance):
                    passing(step, way, distance).wait_send()


def shards(tab, phase, absorb, probe, offsets, measured):
    win = probe.shape[-1]
    obj = phase.shape[-1]
    num_pos = offsets.shape[0]
    sections = lax.axis_size("depth")
    vmem = pl.BlockSpec(memory_space=pltpu.VMEM)
    anywhere = pl.BlockSpec(memory_space=pl.ANY)
    limit = 48 * 1024 * 1024
    groups = lax.axis_size("scan")
    rows = obj // groups
    rounds = sections // LANES // 4
    first = lax.axis_index("scan") * rows
    raw = jnp.concatenate([lax.dynamic_slice_in_dim(values, first, rows, axis=1) for values in (phase, absorb)])
    field, corners = pl.pallas_call(
        gather_kernel,
        out_shape=[
            jax.ShapeDtypeStruct((2, obj + 8, obj), F32),
            jax.ShapeDtypeStruct((groups, 128), jnp.int32),
        ],
        in_specs=[anywhere, vmem],
        out_specs=[vmem, vmem],
        scratch_shapes=[
            pltpu.VMEM((num_pos, 2), jnp.int32),
            pltpu.VMEM((2, rows, obj), F32),
            pltpu.VMEM((num_pos, 128), jnp.int32),
            pltpu.SemaphoreType.DMA,
            pltpu.SemaphoreType.DMA((2,)),
            pltpu.SemaphoreType.DMA((groups,)),
            pltpu.SemaphoreType.DMA((groups,)),
            pltpu.SemaphoreType.DMA((2, rounds, 2)),
            pltpu.SemaphoreType.DMA((2, rounds, 2)),
        ],
        compiler_params=pltpu.CompilerParams(
            collective_id=2, has_side_effects=True, vmem_limit_bytes=48 * 1024 * 1024),
    )(offsets, raw)
    windows = pl.pallas_call(
        window_kernel,
        out_shape=jax.ShapeDtypeStruct((num_pos, 2, win, win), F32),
        in_specs=[vmem, vmem],
        out_specs=vmem,
        scratch_shapes=[pltpu.SMEM((groups, 128), jnp.int32), pltpu.SemaphoreType.DMA],
        compiler_params=pltpu.CompilerParams(vmem_limit_bytes=limit),
    )(corners, field)
    got = pl.pallas_call(
        functools.partial(chain_kernel, sections, num_pos),
        out_shape=jax.ShapeDtypeStruct((num_pos, 2, win, win), F32),
        in_specs=[vmem, anywhere, anywhere, anywhere],
        out_specs=vmem,
        scratch_shapes=[
            pltpu.VMEM((sections, 2, win, win), F32),
            pltpu.VMEM((sections, 2, win, win), F32),
            pltpu.VMEM((2, win, win), F32),
            pltpu.VMEM((win, win), F32),
            pltpu.VMEM(tab.shape, BF16),
            pltpu.SemaphoreType.DMA((3,)),
            pltpu.SemaphoreType.REGULAR,
            pltpu.SemaphoreType.DMA((num_pos,)),
            pltpu.SemaphoreType.DMA((sections,)),
            pltpu.SemaphoreType.DMA((sections,)),
            pltpu.SemaphoreType.DMA((num_pos,)),
        ],
        compiler_params=pltpu.CompilerParams(
            collective_id=0, has_side_effects=True, vmem_limit_bytes=limit),
    )(windows, probe, measured, tab)
    fields = pl.pallas_call(
        field_kernel,
        out_shape=jax.ShapeDtypeStruct((2, obj + 8, obj), F32),
        in_specs=[vmem, vmem],
        out_specs=vmem,
        scratch_shapes=[pltpu.SMEM((groups, 128), jnp.int32), pltpu.SemaphoreType.DMA],
        compiler_params=pltpu.CompilerParams(vmem_limit_bytes=limit),
    )(corners, got)
    return pl.pallas_call(
        sum_kernel,
        out_shape=[jax.ShapeDtypeStruct((1, rows, obj), F32)] * 2,
        in_specs=[vmem],
        out_specs=[vmem, vmem],
        scratch_shapes=[
            pltpu.VMEM((2, rounds, 2, 2, rows, obj), F32),
            pltpu.VMEM((2, rounds - 1, 2, rows, obj), F32),
            pltpu.VMEM((2, 2, rows, obj), F32),
            pltpu.SemaphoreType.DMA((2,)),
            pltpu.SemaphoreType.DMA((2, rounds, 2)),
            pltpu.SemaphoreType.DMA((2, rounds, 2)),
        ],
        compiler_params=pltpu.CompilerParams(
            collective_id=1, has_side_effects=True, vmem_limit_bytes=limit),
    )(fields)


def solution(mesh):
    tab = tables(128)
    in_specs = (
        P("depth", None, None),
        P("depth", None, None),
        P(),
        P("scan", None),
        P("scan", None, None),
    )
    out_specs = (P("depth", "scan", None), P("depth", "scan", None))

    def run(phase, absorb, probe, offsets, measured):
        body = functools.partial(shards, jnp.asarray(tab))
        return jax.shard_map(body, mesh=mesh, in_specs=in_specs, out_specs=out_specs, check_vma=False)(
            phase, absorb, probe, offsets, measured)

    return run
```

```python
import functools

import jax
import jax.numpy as jnp
import ml_dtypes
import numpy as np
from jax import lax
from jax.experimental import pallas as pl
from jax.experimental.pallas import tpu as pltpu
from jax.sharding import PartitionSpec as P

MESH = pl.DeviceIdType.MESH
BF16 = jnp.bfloat16
F32 = jnp.float32
LANES = 2
SIDE = 4
AHEAD = 13


def tables(win):
    idx = np.arange(win)
    ang = 2.0 * np.pi * (np.outer(idx, idx) % win) / win
    fwd = np.exp(-1j * ang) / np.sqrt(win)
    signed = np.where(idx < win // 2, idx, idx - win).astype(np.float64)
    chirp = np.exp(-1j * signed**2 / win)
    prop = np.conj(fwd) @ (chirp[:, None] * fwd)
    prop = 0.5 * (prop + prop.T)
    out = []
    for mat in (prop, fwd):
        right = np.block([[mat.real, mat.imag], [-mat.imag, mat.real]])
        left = np.block([[mat.real, -mat.imag], [mat.imag, mat.real]])
        for block in (right, left):
            block = block.astype(np.float32)
            high = block.astype(ml_dtypes.bfloat16)
            low = (block - high.astype(np.float32)).astype(ml_dtypes.bfloat16)
            out += [high, low]
    return np.stack(out)


def split(values):
    high = values.astype(BF16)
    low = (values - high.astype(F32)).astype(BF16)
    return high, low


def sandwich(re, im, tab, right, left):
    win = re.shape[0]
    high, low = split(jnp.concatenate([re, im], axis=1))
    both = jnp.concatenate([high, low], axis=0)
    main = jnp.dot(both, tab[right], preferred_element_type=F32)
    half = main[:win] + main[win:] + jnp.dot(high, tab[right + 1], preferred_element_type=F32)
    high, low = split(jnp.concatenate([half[:, :win], half[:, win:]], axis=0))
    both = jnp.concatenate([high, low], axis=1)
    main = jnp.dot(tab[left], both, preferred_element_type=F32)
    done = main[:, :win] + main[:, win:] + jnp.dot(tab[left + 1], high, preferred_element_type=F32)
    return done[:win], done[win:]


def turned(index):
    first, last = lax.div(index, 8), lax.rem(index, 2)
    return index + 7 * (last - first)


def place():
    depth = lax.axis_index("depth")
    return lax.axis_index("scan"), lax.div(depth, LANES), lax.rem(depth, LANES)


def home(j, z):
    scan = 2 * j + lax.rem(z, 2)
    return scan, LANES * z + lax.rem(lax.div(scan, SIDE), 2)


def corner(off_ref, j):
    z = lax.div(lax.axis_index("depth"), LANES)
    scan = 2 * j + lax.rem(z, 2)
    return off_ref[scan, 0], off_ref[scan, 1]


def around(scan, z, lane, planes, distance):
    return scan, LANES * lax.rem(z + planes + distance, planes) + lane


def strip_rows(z, rows):
    return pl.ds(pl.multiple_of(turned(z) * rows, 8), rows)


def gather_kernel(
    off_ref, raw, field_ref, corner_ref,
    near_off, made, line, off_sem, turn_sem, line_send, line_recv, send_sem, recv_sem,
):
    scan, z, lane = place()
    groups = lax.axis_size("scan")
    planes = lax.axis_size("depth") // LANES
    rows = made.shape[1]
    rounds = planes // 4
    fetch = pltpu.make_async_copy(off_ref, near_off, off_sem)
    fetch.start()
    to = (turned(z), LANES * turned(scan) + lane)
    stays = turned(z) == scan
    near = (-2, -1, 1, 2)

    barrier = pltpu.get_barrier_semaphore()
    for distance in near:
        pl.semaphore_signal(
            barrier, inc=1, device_id=around(scan, z, lane, planes, distance), device_id_type=MESH)

    @pl.when(jnp.logical_not(stays))
    def _():
        pl.semaphore_signal(barrier, inc=1, device_id=to, device_id_type=MESH)

    def greet(step, carry):
        other = (lax.rem(scan + step, groups), LANES * z + lane)
        pl.semaphore_signal(barrier, inc=1, device_id=other, device_id_type=MESH)
        return carry

    lax.fori_loop(1, groups, greet, 0)
    line[...] = jnp.zeros_like(line)
    field_ref[:, groups * rows :] = jnp.zeros((2, field_ref.shape[1] - groups * rows, field_ref.shape[2]), F32)
    fetch.wait()
    line[:, : near_off.shape[1]] = near_off[...]
    amp = jnp.exp(-raw[1])
    made[0] = amp * jnp.cos(raw[0])
    made[1] = amp * jnp.sin(raw[0])

    def turn(part):
        return pltpu.make_async_remote_copy(
            src_ref=made.at[part], dst_ref=field_ref.at[part, strip_rows(turned(scan), rows), :],
            send_sem=turn_sem.at[0, part], recv_sem=turn_sem.at[1, part], device_id=to, device_id_type=MESH)

    def stay(part):
        return pltpu.make_async_copy(
            made.at[part], field_ref.at[part, strip_rows(z, rows), :], turn_sem.at[1, part])

    @pl.when(stays)
    def _():
        pl.semaphore_wait(barrier, len(near) + groups - 1)
        for part in range(2):
            stay(part).start()

    @pl.when(jnp.logical_not(stays))
    def _():
        pl.semaphore_wait(barrier, len(near) + groups)
        for part in range(2):
            turn(part).start()

    own_line = line.at[pl.ds(lax.div(z, 2), 1), :]
    own = pltpu.make_async_copy(own_line, corner_ref.at[pl.ds(scan, 1), :], line_recv.at[scan])
    own.start()

    def tell(step):
        return pltpu.make_async_remote_copy(
            src_ref=own_line, dst_ref=corner_ref.at[pl.ds(scan, 1), :],
            send_sem=line_send.at[step], recv_sem=line_recv.at[scan],
            device_id=(lax.rem(scan + step, groups), LANES * z + lane), device_id_type=MESH)

    def start_tell(step, carry):
        tell(step).start()
        return carry

    lax.fori_loop(1, groups, start_tell, 0)

    def passing(step, way, distance, part):
        sign = 1 if way == 0 else -1
        whose = lax.rem(z + planes - sign * 2 * step, planes)
        block = field_ref.at[part, strip_rows(whose, rows), :]
        return pltpu.make_async_remote_copy(
            src_ref=block, dst_ref=block,
            send_sem=send_sem.at[way, step, distance - 1, part], recv_sem=recv_sem.at[way, step, distance - 1, part],
            device_id=around(scan, z, lane, planes, sign * distance), device_id_type=MESH)

    def goes(step, way, distance):
        return not (way == 1 and step == rounds - 1 and distance == 2)

    plan = [(step, way, distance, part)
            for step in range(rounds) for part in range(2) for distance in (2, 1) for way in range(2)
            if goes(step, way, distance)]
    for step, way, distance, part in plan:
        if step == 0 and distance == 2 and way == 0:
            stay(part).wait()
        if step > 0 and (distance == 2 or not goes(step, way, 2)):
            passing(step - 1, way, 2, part).wait_recv()
        passing(step, way, distance, part).start()
    for part in range(2):
        passing(rounds - 1, 0, 2, part).wait_recv()
    for step, way, distance, part in plan:
        if distance == 1:
            passing(step, way, distance, part).wait_recv()
    for step, way, distance, part in plan:
        passing(step, way, distance, part).wait_send()

    @pl.when(jnp.logical_not(stays))
    def _():
        for part in range(2):
            turn(part).wait_send()

    def end_tell(step, carry):
        one = lax.rem(scan + step, groups)
        pltpu.make_async_copy(own_line, corner_ref.at[pl.ds(one, 1), :], line_recv.at[one]).wait()

        @pl.when(step > 0)
        def _():
            tell(step).wait_send()
        return carry

    lax.fori_loop(0, groups, end_tell, 0)


def window_kernel(corner_ref, field_ref, out_ref, off_ref, off_sem):
    win = out_ref.shape[-1]
    fetch = pltpu.make_async_copy(corner_ref, off_ref, off_sem)
    fetch.start()
    fetch.wait()

    def one(j, carry):
        row, col = corner(off_ref, j)
        high = lax.div(row, 8)
        low = row - 8 * high
        side = lax.min(lax.div(col, win), 1)
        tall = pl.ds(pl.multiple_of(8 * high, 8), win + 8)
        wide = pl.ds(pl.multiple_of(win * side, win), 2 * win)
        for part in range(2):
            rows = field_ref[part, tall, wide]
            cols = pltpu.roll(rows, lax.rem(2 * win - (col - win * side), 2 * win), 1)[:, :win]
            out_ref[j, part] = pltpu.roll(cols, lax.rem(win + 8 - low, win + 8), 0)[:win]
        return carry

    lax.fori_loop(0, out_ref.shape[0], one, 0)


def field_kernel(corner_ref, got_ref, out_ref, off_ref, off_sem):
    win = got_ref.shape[-1]
    fetch = pltpu.make_async_copy(corner_ref, off_ref, off_sem)
    fetch.start()
    out_ref[...] = jnp.zeros_like(out_ref)
    fetch.wait()

    def one(j, carry):
        row, col = corner(off_ref, j)
        high = lax.div(row, 8)
        low = row - 8 * high
        side = lax.min(lax.div(col, win), 1)
        tall = pl.ds(pl.multiple_of(8 * high, 8), win + 8)
        wide = pl.ds(pl.multiple_of(win * side, win), 2 * win)
        for part in range(2):
            block = jnp.concatenate([got_ref[j, part], jnp.zeros((8, win), F32)], axis=0)
            block = pltpu.roll(block, low, 0)
            block = jnp.concatenate([block, jnp.zeros((win + 8, win), F32)], axis=1)
            out_ref[part, tall, wide] += pltpu.roll(block, col - win * side, 1)
        return carry

    lax.fori_loop(0, got_ref.shape[0], one, 0)


def chain_kernel(
    sections, num_pos, tw_ref, probe_ref, all_meas_ref, all_tab_ref, got_ref,
    trans, exits, wave, meas_ref, tab_ref, load_sem, go_sem, win_send, win_recv, grad_send, grad_recv,
):
    scan, z, lane = place()
    depth = LANES * z + lane
    mine = 2 * turned(scan) + lane
    slot = lax.div(z, 2)
    member = lax.div(scan, 2)

    def is_home(on_scan, on_lane):
        return jnp.logical_and(lax.rem(on_scan, 2) == lax.rem(z, 2), on_lane == lax.rem(lax.div(on_scan, SIDE), 2))

    active = is_home(scan, lane)

    def owner(k):
        return turned(lax.div(k, LANES)), LANES * z + lax.rem(k, LANES)

    loads = [
        pltpu.make_async_copy(src, dst, load_sem.at[i])
        for i, (src, dst) in enumerate(
            ((probe_ref, wave), (all_meas_ref.at[slot], meas_ref), (all_tab_ref, tab_ref)))
    ]
    for load in loads:
        load.start()
    barrier = pltpu.get_barrier_semaphore()

    @pl.when(active)
    def _():
        def greet(k, carry):
            @pl.when(k != mine)
            def _():
                pl.semaphore_signal(barrier, inc=1, device_id=owner(k), device_id_type=MESH)
            return carry
        lax.fori_loop(0, sections, greet, 0)

    @pl.when(jnp.logical_not(active))
    def _():
        def greet(j, carry):
            pl.semaphore_signal(barrier, inc=1, device_id=home(j, z), device_id_type=MESH)
            return carry
        lax.fori_loop(0, num_pos, greet, 0)

    @pl.when(active)
    def _():
        pl.semaphore_wait(barrier, sections - 1)

    @pl.when(jnp.logical_not(active))
    def _():
        pl.semaphore_wait(barrier, num_pos)

    def is_here(j):
        return jnp.logical_and(active, j == member)

    def window_copy(j):
        return pltpu.make_async_remote_copy(
            src_ref=tw_ref.at[j], dst_ref=trans.at[mine], send_sem=win_send.at[j], recv_sem=win_recv.at[mine],
            device_id=home(j, z), device_id_type=MESH)

    def send_window(step, carry):
        j = lax.rem(step + member, num_pos)
        here = is_here(j)

        @pl.when(jnp.logical_not(here))
        def _():
            window_copy(j).start()

        @pl.when(here)
        def _():
            pltpu.make_async_copy(tw_ref.at[j], trans.at[mine], win_recv.at[mine]).start()
        return carry

    def send_windows():
        lax.fori_loop(0, num_pos, send_window, 0)

    @pl.when(mine < AHEAD)
    def _():
        send_windows()

    @pl.when(jnp.logical_and(jnp.logical_not(active), mine >= AHEAD))
    def _():
        pl.semaphore_wait(go_sem, 1)
        send_windows()

    def call_up(k):
        @pl.when(jnp.logical_and(k == mine, k >= AHEAD))
        def _():
            send_windows()

        to, on_plane = owner(k)
        on_lane = on_plane - LANES * z
        awaits = jnp.logical_not(is_home(to, on_lane))
        chosen = jnp.logical_and(lax.rem(k, num_pos) == member, k < sections)

        @pl.when(jnp.logical_and(awaits, chosen))
        def _():
            pl.semaphore_signal(go_sem, inc=1, device_id=owner(k), device_id_type=MESH)

    def grad_copy(k):
        return pltpu.make_async_remote_copy(
            src_ref=exits.at[k], dst_ref=got_ref.at[member], send_sem=grad_send.at[k],
            recv_sem=grad_recv.at[member], device_id=owner(k), device_id_type=MESH)

    for load in loads:
        load.wait()

    @pl.when(active)
    def _():
        def step_in(k):
            pltpu.make_async_copy(tw_ref.at[0], trans.at[k], win_recv.at[k]).wait()
            tr, ti = trans[k, 0], trans[k, 1]
            wr, wi = wave[0], wave[1]
            er = wr * tr - wi * ti
            ei = wr * ti + wi * tr
            exits[k, 0] = er
            exits[k, 1] = ei
            return er, ei

        def forward(k, carry):
            call_up(k + AHEAD)
            er, ei = step_in(k)
            wr, wi = sandwich(er, ei, tab_ref, 0, 2)
            wave[0] = wr
            wave[1] = wi
            return carry

        lax.fori_loop(0, sections - 1, forward, 0, unroll=2)
        er, ei = step_in(sections - 1)
        fr, fi = sandwich(er, ei, tab_ref, 4, 6)
        resid = fr * fr + fi * fi - meas_ref[...]
        lr, li = sandwich(resid * fr, resid * fi, tab_ref, 6, 4)
        wave[0] = lr
        wave[1] = li

        def grads(k):
            er, ei = exits[k, 0], exits[k, 1]
            lr, li = wave[0], wave[1]
            exits[k, 0] = er * li - ei * lr
            exits[k, 1] = -(er * lr + ei * li)

            @pl.when(k != mine)
            def _():
                grad_copy(k).start()

            @pl.when(k == mine)
            def _():
                pltpu.make_async_copy(exits.at[k], got_ref.at[member], grad_recv.at[member]).start()
            return lr, li

        def backward(j, carry):
            k = sections - 1 - j
            lr, li = grads(k)
            tr, ti = trans[k, 0], trans[k, 1]
            wr, wi = sandwich(tr * lr + ti * li, tr * li - ti * lr, tab_ref, 2, 0)
            wave[0] = wr
            wave[1] = wi
            return carry

        lax.fori_loop(0, sections - 1, backward, 0, unroll=2)
        grads(0)

    def finish(j, carry):
        @pl.when(jnp.logical_not(is_here(j)))
        def _():
            window_copy(j).wait_send()
        pltpu.make_async_copy(tw_ref.at[0], got_ref.at[j], grad_recv.at[j]).wait()
        return carry

    lax.fori_loop(0, num_pos, finish, 0)

    @pl.when(active)
    def _():
        def drain(k, carry):
            @pl.when(k != mine)
            def _():
                grad_copy(k).wait_send()
            return carry
        lax.fori_loop(0, sections, drain, 0)


def sum_kernel(parts_ref, both_ref, got, made, last, turn_sem, send_sem, recv_sem):
    scan, z, lane = place()
    planes = lax.axis_size("depth") // LANES
    rows = last.shape[2]
    rounds = planes // 4
    to = (turned(z), LANES * turned(scan) + lane)
    stays = turned(z) == scan
    near = (-2, -1, 1, 2)
    barrier = pltpu.get_barrier_semaphore()
    for distance in near:
        pl.semaphore_signal(
            barrier, inc=1, device_id=around(scan, z, lane, planes, distance), device_id_type=MESH)

    @pl.when(jnp.logical_not(stays))
    def _():
        pl.semaphore_signal(barrier, inc=1, device_id=to, device_id_type=MESH)
        pl.semaphore_wait(barrier, len(near) + 1)

    @pl.when(stays)
    def _():
        pl.semaphore_wait(barrier, len(near))

    def strip(way, ahead, part):
        sign = 1 if way == 0 else -1
        return parts_ref.at[part, strip_rows(lax.rem(z + planes + sign * ahead, planes), rows), :]

    def goes(step, way, distance):
        return not (way == 1 and step == 0 and distance == 2)

    def passing(step, way, distance, part):
        ahead = planes // 2 - 2 * step - (2 - distance)
        bare = distance == 1 or step == 0
        return pltpu.make_async_remote_copy(
            src_ref=strip(way, ahead, part) if bare else made.at[way, step - 1, part],
            dst_ref=got.at[way, step, distance - 1, part],
            send_sem=send_sem.at[way, step, distance - 1, part],
            recv_sem=recv_sem.at[way, step, distance - 1, part],
            device_id=around(scan, z, lane, planes, distance if way == 0 else -distance), device_id_type=MESH)

    def arrived(step, way, part):
        passing(step, way, 1, part).wait_recv()
        total = got[way, step, 0, part]
        if goes(step, way, 2):
            passing(step, way, 2, part).wait_recv()
            total = total + got[way, step, 1, part]
        return total

    for part in range(2):
        for way in range(2):
            if goes(0, way, 2):
                passing(0, way, 2, part).start()
        for way in range(2):
            passing(0, way, 1, part).start()
    for part in range(2):
        for way in range(2):
            passing(1, way, 1, part).start()
    for step in range(1, rounds):
        for part in range(2):
            for way in range(2):
                ahead = planes // 2 - 2 * step
                made[way, step - 1, part] = strip(way, ahead, part)[...] + arrived(step - 1, way, part)
                passing(step, way, 2, part).start()
            if step + 1 < rounds:
                for way in range(2):
                    passing(step + 1, way, 1, part).start()

    def turn(part):
        return pltpu.make_async_remote_copy(
            src_ref=last.at[0, part], dst_ref=last.at[1, part],
            send_sem=turn_sem.at[0, part], recv_sem=turn_sem.at[1, part],
            device_id=to, device_id_type=MESH)

    for part in range(2):
        total = strip(0, 0, part)[...] + (arrived(rounds - 1, 0, part) + arrived(rounds - 1, 1, part))
        last[0, part] = total

        @pl.when(jnp.logical_not(stays))
        def _():
            turn(part).start()

    for part in range(2):
        @pl.when(jnp.logical_not(stays))
        def _():
            turn(part).wait()
            both_ref[part] = last[1, part]

        @pl.when(stays)
        def _():
            both_ref[part] = last[0, part]

    for step in range(rounds):
        for way in range(2):
            for distance in (1, 2):
                if goes(step, way, distance):
                    for part in range(2):
                        passing(step, way, distance, part).wait_send()


def shards(tab, phase, absorb, probe, offsets, measured):
    win = probe.shape[-1]
    obj = phase.shape[-1]
    num_pos = offsets.shape[0]
    sections = lax.axis_size("depth")
    vmem = pl.BlockSpec(memory_space=pltpu.VMEM)
    anywhere = pl.BlockSpec(memory_space=pl.ANY)
    limit = 48 * 1024 * 1024
    groups = lax.axis_size("scan")
    rows = obj // groups
    rounds = sections // LANES // 4
    first = lax.axis_index("scan") * rows
    raw = jnp.concatenate([lax.dynamic_slice_in_dim(values, first, rows, axis=1) for values in (phase, absorb)])
    field, corners = pl.pallas_call(
        gather_kernel,
        out_shape=[
            jax.ShapeDtypeStruct((2, obj + 8, obj), F32),
            jax.ShapeDtypeStruct((groups, 128), jnp.int32),
        ],
        in_specs=[anywhere, vmem],
        out_specs=[vmem, vmem],
        scratch_shapes=[
            pltpu.VMEM((num_pos, 2), jnp.int32),
            pltpu.VMEM((2, rows, obj), F32),
            pltpu.VMEM((num_pos, 128), jnp.int32),
            pltpu.SemaphoreType.DMA,
            pltpu.SemaphoreType.DMA((2, 2)),
            pltpu.SemaphoreType.DMA((groups,)),
            pltpu.SemaphoreType.DMA((groups,)),
            pltpu.SemaphoreType.DMA((2, rounds, 2, 2)),
            pltpu.SemaphoreType.DMA((2, rounds, 2, 2)),
        ],
        compiler_params=pltpu.CompilerParams(
            collective_id=2, has_side_effects=True, vmem_limit_bytes=48 * 1024 * 1024),
    )(offsets, raw)
    windows = pl.pallas_call(
        window_kernel,
        out_shape=jax.ShapeDtypeStruct((num_pos, 2, win, win), F32),
        in_specs=[vmem, vmem],
        out_specs=vmem,
        scratch_shapes=[pltpu.SMEM((groups, 128), jnp.int32), pltpu.SemaphoreType.DMA],
        compiler_params=pltpu.CompilerParams(vmem_limit_bytes=limit),
    )(corners, field)
    got = pl.pallas_call(
        functools.partial(chain_kernel, sections, num_pos),
        out_shape=jax.ShapeDtypeStruct((num_pos, 2, win, win), F32),
        in_specs=[vmem, anywhere, anywhere, anywhere],
        out_specs=vmem,
        scratch_shapes=[
            pltpu.VMEM((sections, 2, win, win), F32),
            pltpu.VMEM((sections, 2, win, win), F32),
            pltpu.VMEM((2, win, win), F32),
            pltpu.VMEM((win, win), F32),
            pltpu.VMEM(tab.shape, BF16),
            pltpu.SemaphoreType.DMA((3,)),
            pltpu.SemaphoreType.REGULAR,
            pltpu.SemaphoreType.DMA((num_pos,)),
            pltpu.SemaphoreType.DMA((sections,)),
            pltpu.SemaphoreType.DMA((sections,)),
            pltpu.SemaphoreType.DMA((num_pos,)),
        ],
        compiler_params=pltpu.CompilerParams(
            collective_id=0, has_side_effects=True, vmem_limit_bytes=limit),
    )(windows, probe, measured, tab)
    fields = pl.pallas_call(
        field_kernel,
        out_shape=jax.ShapeDtypeStruct((2, obj + 8, obj), F32),
        in_specs=[vmem, vmem],
        out_specs=vmem,
        scratch_shapes=[pltpu.SMEM((groups, 128), jnp.int32), pltpu.SemaphoreType.DMA],
        compiler_params=pltpu.CompilerParams(vmem_limit_bytes=limit),
    )(corners, got)
    both = pl.pallas_call(
        sum_kernel,
        out_shape=jax.ShapeDtypeStruct((2, rows, obj), F32),
        in_specs=[vmem],
        out_specs=vmem,
        scratch_shapes=[
            pltpu.VMEM((2, rounds, 2, 2, rows, obj), F32),
            pltpu.VMEM((2, rounds - 1, 2, rows, obj), F32),
            pltpu.VMEM((2, 2, rows, obj), F32),
            pltpu.SemaphoreType.DMA((2, 2)),
            pltpu.SemaphoreType.DMA((2, rounds, 2, 2)),
            pltpu.SemaphoreType.DMA((2, rounds, 2, 2)),
        ],
        compiler_params=pltpu.CompilerParams(
            collective_id=1, has_side_effects=True, vmem_limit_bytes=limit),
    )(fields)
    return both[:1], both[1:]


def solution(mesh):
    tab = tables(128)
    in_specs = (
        P("depth", None, None),
        P("depth", None, None),
        P(),
        P("scan", None),
        P("scan", None, None),
    )
    out_specs = (P("depth", "scan", None), P("depth", "scan", None))

    def run(phase, absorb, probe, offsets, measured):
        body = functools.partial(shards, jnp.asarray(tab))
        return jax.shard_map(body, mesh=mesh, in_specs=in_specs, out_specs=out_specs, check_vma=False)(
            phase, absorb, probe, offsets, measured)

    return run
```

```python
import functools

import jax
import jax.numpy as jnp
import ml_dtypes
import numpy as np
from jax import lax
from jax.experimental import pallas as pl
from jax.experimental.pallas import tpu as pltpu
from jax.sharding import PartitionSpec as P

MESH = pl.DeviceIdType.MESH
BF16 = jnp.bfloat16
F32 = jnp.float32
LANES = 2
SIDE = 4
AHEAD = 13


def tables(win):
    idx = np.arange(win)
    ang = 2.0 * np.pi * (np.outer(idx, idx) % win) / win
    fwd = np.exp(-1j * ang) / np.sqrt(win)
    signed = np.where(idx < win // 2, idx, idx - win).astype(np.float64)
    chirp = np.exp(-1j * signed**2 / win)
    prop = np.conj(fwd) @ (chirp[:, None] * fwd)
    prop = 0.5 * (prop + prop.T)
    out = []
    for mat in (prop, fwd):
        right = np.block([[mat.real, mat.imag], [-mat.imag, mat.real]])
        left = np.block([[mat.real, -mat.imag], [mat.imag, mat.real]])
        for block in (right, left):
            block = block.astype(np.float32)
            high = block.astype(ml_dtypes.bfloat16)
            low = (block - high.astype(np.float32)).astype(ml_dtypes.bfloat16)
            out += [high, low]
    return np.stack(out)


def split(values):
    high = values.astype(BF16)
    low = (values - high.astype(F32)).astype(BF16)
    return high, low


def sandwich(re, im, tab, right, left):
    win = re.shape[0]
    high, low = split(jnp.concatenate([re, im], axis=1))
    both = jnp.concatenate([high, low], axis=0)
    main = jnp.dot(both, tab[right], preferred_element_type=F32)
    half = main[:win] + main[win:] + jnp.dot(high, tab[right + 1], preferred_element_type=F32)
    high, low = split(jnp.concatenate([half[:, :win], half[:, win:]], axis=0))
    both = jnp.concatenate([high, low], axis=1)
    main = jnp.dot(tab[left], both, preferred_element_type=F32)
    done = main[:, :win] + main[:, win:] + jnp.dot(tab[left + 1], high, preferred_element_type=F32)
    return done[:win], done[win:]


def turned(index):
    first, last = lax.div(index, 8), lax.rem(index, 2)
    return index + 7 * (last - first)


def place():
    depth = lax.axis_index("depth")
    return lax.axis_index("scan"), lax.div(depth, LANES), lax.rem(depth, LANES)


def home(j, z):
    scan = 2 * j + lax.rem(z, 2)
    return scan, LANES * z + lax.rem(lax.div(scan, SIDE), 2)


def corner(off_ref, j):
    z = lax.div(lax.axis_index("depth"), LANES)
    scan = 2 * j + lax.rem(z, 2)
    return off_ref[scan, 0], off_ref[scan, 1]


def around(scan, z, lane, planes, distance):
    return scan, LANES * lax.rem(z + planes + distance, planes) + lane


def strip_rows(z, rows):
    return pl.ds(pl.multiple_of(turned(z) * rows, 8), rows)


def gather_kernel(
    off_ref, raw, field_ref, corner_ref,
    near_off, made, line, off_sem, turn_sem, line_send, line_recv, send_sem, recv_sem,
):
    scan, z, lane = place()
    groups = lax.axis_size("scan")
    planes = lax.axis_size("depth") // LANES
    rows = made.shape[1]
    rounds = planes // 4
    fetch = pltpu.make_async_copy(off_ref, near_off, off_sem)
    fetch.start()
    to = (turned(z), LANES * turned(scan) + lane)
    stays = turned(z) == scan
    near = (-2, -1, 1, 2)

    barrier = pltpu.get_barrier_semaphore()
    for distance in near:
        pl.semaphore_signal(
            barrier, inc=1, device_id=around(scan, z, lane, planes, distance), device_id_type=MESH)

    @pl.when(jnp.logical_not(stays))
    def _():
        pl.semaphore_signal(barrier, inc=1, device_id=to, device_id_type=MESH)

    def greet(step, carry):
        other = (lax.rem(scan + step, groups), LANES * z + lane)
        pl.semaphore_signal(barrier, inc=1, device_id=other, device_id_type=MESH)
        return carry

    lax.fori_loop(1, groups, greet, 0)
    line[...] = jnp.zeros_like(line)
    field_ref[:, groups * rows :] = jnp.zeros((2, field_ref.shape[1] - groups * rows, field_ref.shape[2]), F32)
    fetch.wait()
    line[:, : near_off.shape[1]] = near_off[...]
    amp = jnp.exp(-raw[1])
    made[0] = amp * jnp.cos(raw[0])
    made[1] = amp * jnp.sin(raw[0])

    def turn(part):
        return pltpu.make_async_remote_copy(
            src_ref=made.at[part], dst_ref=field_ref.at[part, strip_rows(turned(scan), rows), :],
            send_sem=turn_sem.at[0, part], recv_sem=turn_sem.at[1, part], device_id=to, device_id_type=MESH)

    def stay(part):
        return pltpu.make_async_copy(
            made.at[part], field_ref.at[part, strip_rows(z, rows), :], turn_sem.at[1, part])

    @pl.when(stays)
    def _():
        pl.semaphore_wait(barrier, len(near) + groups - 1)
        for part in range(2):
            stay(part).start()

    @pl.when(jnp.logical_not(stays))
    def _():
        pl.semaphore_wait(barrier, len(near) + groups)
        for part in range(2):
            turn(part).start()

    own_line = line.at[pl.ds(lax.div(z, 2), 1), :]
    own = pltpu.make_async_copy(own_line, corner_ref.at[pl.ds(scan, 1), :], line_recv.at[scan])
    own.start()

    def tell(step):
        return pltpu.make_async_remote_copy(
            src_ref=own_line, dst_ref=corner_ref.at[pl.ds(scan, 1), :],
            send_sem=line_send.at[step], recv_sem=line_recv.at[scan],
            device_id=(lax.rem(scan + step, groups), LANES * z + lane), device_id_type=MESH)

    def start_tell(step, carry):
        tell(step).start()
        return carry

    lax.fori_loop(1, groups, start_tell, 0)

    def passing(step, way, distance, part):
        sign = 1 if way == 0 else -1
        whose = lax.rem(z + planes - sign * 2 * step, planes)
        block = field_ref.at[part, strip_rows(whose, rows), :]
        return pltpu.make_async_remote_copy(
            src_ref=block, dst_ref=block,
            send_sem=send_sem.at[way, step, distance - 1, part], recv_sem=recv_sem.at[way, step, distance - 1, part],
            device_id=around(scan, z, lane, planes, sign * distance), device_id_type=MESH)

    def goes(step, way, distance, part):
        return not (way == 1 - part and step == rounds - 1 and distance == 2)

    plan = [(step, way, distance, part)
            for step in range(rounds) for part in range(2) for distance in (2, 1) for way in range(2)
            if goes(step, way, distance, part)]
    for step, way, distance, part in plan:
        if step == 0 and distance == 2 and way == 0:
            stay(part).wait()
        if step > 0 and (distance == 2 or not goes(step, way, 2, part)):
            passing(step - 1, way, 2, part).wait_recv()
        passing(step, way, distance, part).start()
    for part in range(2):
        passing(rounds - 1, part, 2, part).wait_recv()
    for step, way, distance, part in plan:
        if distance == 1:
            passing(step, way, distance, part).wait_recv()
    for step, way, distance, part in plan:
        passing(step, way, distance, part).wait_send()

    @pl.when(jnp.logical_not(stays))
    def _():
        for part in range(2):
            turn(part).wait_send()

    def end_tell(step, carry):
        one = lax.rem(scan + step, groups)
        pltpu.make_async_copy(own_line, corner_ref.at[pl.ds(one, 1), :], line_recv.at[one]).wait()

        @pl.when(step > 0)
        def _():
            tell(step).wait_send()
        return carry

    lax.fori_loop(0, groups, end_tell, 0)


def window_kernel(corner_ref, field_ref, out_ref, off_ref, off_sem):
    win = out_ref.shape[-1]
    fetch = pltpu.make_async_copy(corner_ref, off_ref, off_sem)
    fetch.start()
    fetch.wait()

    def one(j, carry):
        row, col = corner(off_ref, j)
        high = lax.div(row, 8)
        low = row - 8 * high
        side = lax.min(lax.div(col, win), 1)
        tall = pl.ds(pl.multiple_of(8 * high, 8), win + 8)
        wide = pl.ds(pl.multiple_of(win * side, win), 2 * win)
        for part in range(2):
            rows = field_ref[part, tall, wide]
            cols = pltpu.roll(rows, lax.rem(2 * win - (col - win * side), 2 * win), 1)[:, :win]
            out_ref[j, part] = pltpu.roll(cols, lax.rem(win + 8 - low, win + 8), 0)[:win]
        return carry

    lax.fori_loop(0, out_ref.shape[0], one, 0)


def field_kernel(corner_ref, got_ref, out_ref, off_ref, off_sem):
    win = got_ref.shape[-1]
    fetch = pltpu.make_async_copy(corner_ref, off_ref, off_sem)
    fetch.start()
    out_ref[...] = jnp.zeros_like(out_ref)
    fetch.wait()

    def one(j, carry):
        row, col = corner(off_ref, j)
        high = lax.div(row, 8)
        low = row - 8 * high
        side = lax.min(lax.div(col, win), 1)
        tall = pl.ds(pl.multiple_of(8 * high, 8), win + 8)
        wide = pl.ds(pl.multiple_of(win * side, win), 2 * win)
        for part in range(2):
            block = jnp.concatenate([got_ref[j, part], jnp.zeros((8, win), F32)], axis=0)
            block = pltpu.roll(block, low, 0)
            block = jnp.concatenate([block, jnp.zeros((win + 8, win), F32)], axis=1)
            out_ref[part, tall, wide] += pltpu.roll(block, col - win * side, 1)
        return carry

    lax.fori_loop(0, got_ref.shape[0], one, 0)


def chain_kernel(
    sections, num_pos, tw_ref, probe_ref, all_meas_ref, all_tab_ref, got_ref,
    trans, exits, wave, meas_ref, tab_ref, load_sem, go_sem, win_send, win_recv, grad_send, grad_recv,
):
    scan, z, lane = place()
    depth = LANES * z + lane
    mine = 2 * turned(scan) + lane
    slot = lax.div(z, 2)
    member = lax.div(scan, 2)

    def is_home(on_scan, on_lane):
        return jnp.logical_and(lax.rem(on_scan, 2) == lax.rem(z, 2), on_lane == lax.rem(lax.div(on_scan, SIDE), 2))

    active = is_home(scan, lane)

    def owner(k):
        return turned(lax.div(k, LANES)), LANES * z + lax.rem(k, LANES)

    loads = [
        pltpu.make_async_copy(src, dst, load_sem.at[i])
        for i, (src, dst) in enumerate(
            ((probe_ref, wave), (all_meas_ref.at[slot], meas_ref), (all_tab_ref, tab_ref)))
    ]
    for load in loads:
        load.start()
    barrier = pltpu.get_barrier_semaphore()

    @pl.when(active)
    def _():
        def greet(k, carry):
            @pl.when(k != mine)
            def _():
                pl.semaphore_signal(barrier, inc=1, device_id=owner(k), device_id_type=MESH)
            return carry
        lax.fori_loop(0, sections, greet, 0)

    @pl.when(jnp.logical_not(active))
    def _():
        def greet(j, carry):
            pl.semaphore_signal(barrier, inc=1, device_id=home(j, z), device_id_type=MESH)
            return carry
        lax.fori_loop(0, num_pos, greet, 0)

    @pl.when(active)
    def _():
        pl.semaphore_wait(barrier, sections - 1)

    @pl.when(jnp.logical_not(active))
    def _():
        pl.semaphore_wait(barrier, num_pos)

    def is_here(j):
        return jnp.logical_and(active, j == member)

    def window_copy(j):
        return pltpu.make_async_remote_copy(
            src_ref=tw_ref.at[j], dst_ref=trans.at[mine], send_sem=win_send.at[j], recv_sem=win_recv.at[mine],
            device_id=home(j, z), device_id_type=MESH)

    def send_window(step, carry):
        j = lax.rem(step + member, num_pos)
        here = is_here(j)

        @pl.when(jnp.logical_not(here))
        def _():
            window_copy(j).start()

        @pl.when(here)
        def _():
            pltpu.make_async_copy(tw_ref.at[j], trans.at[mine], win_recv.at[mine]).start()
        return carry

    def send_windows():
        lax.fori_loop(0, num_pos, send_window, 0)

    @pl.when(mine < AHEAD)
    def _():
        send_windows()

    @pl.when(jnp.logical_and(jnp.logical_not(active), mine >= AHEAD))
    def _():
        pl.semaphore_wait(go_sem, 1)
        send_windows()

    def call_up(k):
        @pl.when(jnp.logical_and(k == mine, k >= AHEAD))
        def _():
            send_windows()

        to, on_plane = owner(k)
        on_lane = on_plane - LANES * z
        awaits = jnp.logical_not(is_home(to, on_lane))
        chosen = jnp.logical_and(lax.rem(k, num_pos) == member, k < sections)

        @pl.when(jnp.logical_and(awaits, chosen))
        def _():
            pl.semaphore_signal(go_sem, inc=1, device_id=owner(k), device_id_type=MESH)

    def grad_copy(k):
        return pltpu.make_async_remote_copy(
            src_ref=exits.at[k], dst_ref=got_ref.at[member], send_sem=grad_send.at[k],
            recv_sem=grad_recv.at[member], device_id=owner(k), device_id_type=MESH)

    for load in loads:
        load.wait()

    @pl.when(active)
    def _():
        def step_in(k):
            pltpu.make_async_copy(tw_ref.at[0], trans.at[k], win_recv.at[k]).wait()
            tr, ti = trans[k, 0], trans[k, 1]
            wr, wi = wave[0], wave[1]
            er = wr * tr - wi * ti
            ei = wr * ti + wi * tr
            exits[k, 0] = er
            exits[k, 1] = ei
            return er, ei

        def forward(k, carry):
            call_up(k + AHEAD)
            er, ei = step_in(k)
            wr, wi = sandwich(er, ei, tab_ref, 0, 2)
            wave[0] = wr
            wave[1] = wi
            return carry

        lax.fori_loop(0, sections - 1, forward, 0, unroll=4)
        er, ei = step_in(sections - 1)
        fr, fi = sandwich(er, ei, tab_ref, 4, 6)
        resid = fr * fr + fi * fi - meas_ref[...]
        lr, li = sandwich(resid * fr, resid * fi, tab_ref, 6, 4)
        wave[0] = lr
        wave[1] = li

        def grads(k):
            er, ei = exits[k, 0], exits[k, 1]
            lr, li = wave[0], wave[1]
            exits[k, 0] = er * li - ei * lr
            exits[k, 1] = -(er * lr + ei * li)

            @pl.when(k != mine)
            def _():
                grad_copy(k).start()

            @pl.when(k == mine)
            def _():
                pltpu.make_async_copy(exits.at[k], got_ref.at[member], grad_recv.at[member]).start()
            return lr, li

        def backward(j, carry):
            k = sections - 1 - j
            lr, li = grads(k)
            tr, ti = trans[k, 0], trans[k, 1]
            wr, wi = sandwich(tr * lr + ti * li, tr * li - ti * lr, tab_ref, 2, 0)
            wave[0] = wr
            wave[1] = wi
            return carry

        lax.fori_loop(0, sections - 1, backward, 0, unroll=4)
        grads(0)

    def finish(j, carry):
        @pl.when(jnp.logical_not(is_here(j)))
        def _():
            window_copy(j).wait_send()
        pltpu.make_async_copy(tw_ref.at[0], got_ref.at[j], grad_recv.at[j]).wait()
        return carry

    lax.fori_loop(0, num_pos, finish, 0)

    @pl.when(active)
    def _():
        def drain(k, carry):
            @pl.when(k != mine)
            def _():
                grad_copy(k).wait_send()
            return carry
        lax.fori_loop(0, sections, drain, 0)


def sum_kernel(parts_ref, both_ref, got, made, last, turn_sem, send_sem, recv_sem):
    scan, z, lane = place()
    planes = lax.axis_size("depth") // LANES
    rows = last.shape[2]
    rounds = planes // 4
    to = (turned(z), LANES * turned(scan) + lane)
    stays = turned(z) == scan
    near = (-2, -1, 1, 2)
    barrier = pltpu.get_barrier_semaphore()
    for distance in near:
        pl.semaphore_signal(
            barrier, inc=1, device_id=around(scan, z, lane, planes, distance), device_id_type=MESH)

    @pl.when(jnp.logical_not(stays))
    def _():
        pl.semaphore_signal(barrier, inc=1, device_id=to, device_id_type=MESH)
        pl.semaphore_wait(barrier, len(near) + 1)

    @pl.when(stays)
    def _():
        pl.semaphore_wait(barrier, len(near))

    def strip(way, ahead, part):
        sign = 1 if way == 0 else -1
        return parts_ref.at[part, strip_rows(lax.rem(z + planes + sign * ahead, planes), rows), :]

    def goes(step, way, distance, part):
        return not (way == 1 - part and step == 0 and distance == 2)

    def passing(step, way, distance, part):
        ahead = planes // 2 - 2 * step - (2 - distance)
        bare = distance == 1 or step == 0
        return pltpu.make_async_remote_copy(
            src_ref=strip(way, ahead, part) if bare else made.at[way, step - 1, part],
            dst_ref=got.at[way, step, distance - 1, part],
            send_sem=send_sem.at[way, step, distance - 1, part],
            recv_sem=recv_sem.at[way, step, distance - 1, part],
            device_id=around(scan, z, lane, planes, distance if way == 0 else -distance), device_id_type=MESH)

    def arrived(step, way, part):
        passing(step, way, 1, part).wait_recv()
        total = got[way, step, 0, part]
        if goes(step, way, 2, part):
            passing(step, way, 2, part).wait_recv()
            total = total + got[way, step, 1, part]
        return total

    for part in range(2):
        for way in range(2):
            if goes(0, way, 2, part):
                passing(0, way, 2, part).start()
        for way in range(2):
            passing(0, way, 1, part).start()
    for part in range(2):
        for way in range(2):
            passing(1, way, 1, part).start()
    for step in range(1, rounds):
        for part in range(2):
            for way in range(2):
                ahead = planes // 2 - 2 * step
                made[way, step - 1, part] = strip(way, ahead, part)[...] + arrived(step - 1, way, part)
                passing(step, way, 2, part).start()
            if step + 1 < rounds:
                for way in range(2):
                    passing(step + 1, way, 1, part).start()

    def turn(part):
        return pltpu.make_async_remote_copy(
            src_ref=last.at[0, part], dst_ref=last.at[1, part],
            send_sem=turn_sem.at[0, part], recv_sem=turn_sem.at[1, part],
            device_id=to, device_id_type=MESH)

    for part in range(2):
        total = strip(0, 0, part)[...] + (arrived(rounds - 1, 0, part) + arrived(rounds - 1, 1, part))
        last[0, part] = total

        @pl.when(jnp.logical_not(stays))
        def _():
            turn(part).start()

    for part in range(2):
        @pl.when(jnp.logical_not(stays))
        def _():
            turn(part).wait()
            both_ref[part] = last[1, part]

        @pl.when(stays)
        def _():
            both_ref[part] = last[0, part]

    for step in range(rounds):
        for way in range(2):
            for distance in (1, 2):
                for part in range(2):
                    if goes(step, way, distance, part):
                        passing(step, way, distance, part).wait_send()


def shards(tab, phase, absorb, probe, offsets, measured):
    win = probe.shape[-1]
    obj = phase.shape[-1]
    num_pos = offsets.shape[0]
    sections = lax.axis_size("depth")
    vmem = pl.BlockSpec(memory_space=pltpu.VMEM)
    anywhere = pl.BlockSpec(memory_space=pl.ANY)
    limit = 48 * 1024 * 1024
    groups = lax.axis_size("scan")
    rows = obj // groups
    rounds = sections // LANES // 4
    first = lax.axis_index("scan") * rows
    raw = jnp.concatenate([lax.dynamic_slice_in_dim(values, first, rows, axis=1) for values in (phase, absorb)])
    field, corners = pl.pallas_call(
        gather_kernel,
        out_shape=[
            jax.ShapeDtypeStruct((2, obj + 8, obj), F32),
            jax.ShapeDtypeStruct((groups, 128), jnp.int32),
        ],
        in_specs=[anywhere, vmem],
        out_specs=[vmem, vmem],
        scratch_shapes=[
            pltpu.VMEM((num_pos, 2), jnp.int32),
            pltpu.VMEM((2, rows, obj), F32),
            pltpu.VMEM((num_pos, 128), jnp.int32),
            pltpu.SemaphoreType.DMA,
            pltpu.SemaphoreType.DMA((2, 2)),
            pltpu.SemaphoreType.DMA((groups,)),
            pltpu.SemaphoreType.DMA((groups,)),
            pltpu.SemaphoreType.DMA((2, rounds, 2, 2)),
            pltpu.SemaphoreType.DMA((2, rounds, 2, 2)),
        ],
        compiler_params=pltpu.CompilerParams(
            collective_id=2, has_side_effects=True, vmem_limit_bytes=48 * 1024 * 1024),
    )(offsets, raw)
    windows = pl.pallas_call(
        window_kernel,
        out_shape=jax.ShapeDtypeStruct((num_pos, 2, win, win), F32),
        in_specs=[vmem, vmem],
        out_specs=vmem,
        scratch_shapes=[pltpu.SMEM((groups, 128), jnp.int32), pltpu.SemaphoreType.DMA],
        compiler_params=pltpu.CompilerParams(vmem_limit_bytes=limit),
    )(corners, field)
    got = pl.pallas_call(
        functools.partial(chain_kernel, sections, num_pos),
        out_shape=jax.ShapeDtypeStruct((num_pos, 2, win, win), F32),
        in_specs=[vmem, anywhere, anywhere, anywhere],
        out_specs=vmem,
        scratch_shapes=[
            pltpu.VMEM((sections, 2, win, win), F32),
            pltpu.VMEM((sections, 2, win, win), F32),
            pltpu.VMEM((2, win, win), F32),
            pltpu.VMEM((win, win), F32),
            pltpu.VMEM(tab.shape, BF16),
            pltpu.SemaphoreType.DMA((3,)),
            pltpu.SemaphoreType.REGULAR,
            pltpu.SemaphoreType.DMA((num_pos,)),
            pltpu.SemaphoreType.DMA((sections,)),
            pltpu.SemaphoreType.DMA((sections,)),
            pltpu.SemaphoreType.DMA((num_pos,)),
        ],
        compiler_params=pltpu.CompilerParams(
            collective_id=0, has_side_effects=True, vmem_limit_bytes=limit),
    )(windows, probe, measured, tab)
    fields = pl.pallas_call(
        field_kernel,
        out_shape=jax.ShapeDtypeStruct((2, obj + 8, obj), F32),
        in_specs=[vmem, vmem],
        out_specs=vmem,
        scratch_shapes=[pltpu.SMEM((groups, 128), jnp.int32), pltpu.SemaphoreType.DMA],
        compiler_params=pltpu.CompilerParams(vmem_limit_bytes=limit),
    )(corners, got)
    both = pl.pallas_call(
        sum_kernel,
        out_shape=jax.ShapeDtypeStruct((2, rows, obj), F32),
        in_specs=[vmem],
        out_specs=vmem,
        scratch_shapes=[
            pltpu.VMEM((2, rounds, 2, 2, rows, obj), F32),
            pltpu.VMEM((2, rounds - 1, 2, rows, obj), F32),
            pltpu.VMEM((2, 2, rows, obj), F32),
            pltpu.SemaphoreType.DMA((2, 2)),
            pltpu.SemaphoreType.DMA((2, rounds, 2, 2)),
            pltpu.SemaphoreType.DMA((2, rounds, 2, 2)),
        ],
        compiler_params=pltpu.CompilerParams(
            collective_id=1, has_side_effects=True, vmem_limit_bytes=limit),
    )(fields)
    return both[:1], both[1:]


def solution(mesh):
    tab = tables(128)
    in_specs = (
        P("depth", None, None),
        P("depth", None, None),
        P(),
        P("scan", None),
        P("scan", None, None),
    )
    out_specs = (P("depth", "scan", None), P("depth", "scan", None))

    def run(phase, absorb, probe, offsets, measured):
        body = functools.partial(shards, jnp.asarray(tab))
        return jax.shard_map(body, mesh=mesh, in_specs=in_specs, out_specs=out_specs, check_vma=False)(
            phase, absorb, probe, offsets, measured)

    return run
```

```python
import functools

import jax
import jax.numpy as jnp
import ml_dtypes
import numpy as np
from jax import lax
from jax.experimental import pallas as pl
from jax.experimental.pallas import tpu as pltpu
from jax.sharding import PartitionSpec as P

MESH = pl.DeviceIdType.MESH
BF16 = jnp.bfloat16
F32 = jnp.float32
LANES = 2
SIDE = 4
AHEAD = 13


def tables(win):
    idx = np.arange(win)
    ang = 2.0 * np.pi * (np.outer(idx, idx) % win) / win
    fwd = np.exp(-1j * ang) / np.sqrt(win)
    signed = np.where(idx < win // 2, idx, idx - win).astype(np.float64)
    chirp = np.exp(-1j * signed**2 / win)
    prop = np.conj(fwd) @ (chirp[:, None] * fwd)
    prop = 0.5 * (prop + prop.T)
    out = []
    for mat in (prop, fwd):
        right = np.block([[mat.real, mat.imag], [-mat.imag, mat.real]])
        left = np.block([[mat.real, -mat.imag], [mat.imag, mat.real]])
        for block in (right, left):
            block = block.astype(np.float32)
            high = block.astype(ml_dtypes.bfloat16)
            low = (block - high.astype(np.float32)).astype(ml_dtypes.bfloat16)
            out += [high, low]
    return np.stack(out)


def split(values):
    high = values.astype(BF16)
    low = (values - high.astype(F32)).astype(BF16)
    return high, low


def sandwich(re, im, tab, right, left):
    win = re.shape[0]
    high, low = split(jnp.concatenate([re, im], axis=1))
    both = jnp.concatenate([high, low], axis=0)
    main = jnp.dot(both, tab[right], preferred_element_type=F32)
    half = main[:win] + main[win:] + jnp.dot(high, tab[right + 1], preferred_element_type=F32)
    high, low = split(jnp.concatenate([half[:, :win], half[:, win:]], axis=0))
    both = jnp.concatenate([high, low], axis=1)
    main = jnp.dot(tab[left], both, preferred_element_type=F32)
    done = main[:, :win] + main[:, win:] + jnp.dot(tab[left + 1], high, preferred_element_type=F32)
    return done[:win], done[win:]


def turned(index):
    first, last = lax.div(index, 8), lax.rem(index, 2)
    return index + 7 * (last - first)


def place():
    depth = lax.axis_index("depth")
    return lax.axis_index("scan"), lax.div(depth, LANES), lax.rem(depth, LANES)


def home(j, z):
    scan = 2 * j + lax.rem(z, 2)
    return scan, LANES * z + lax.rem(lax.div(scan, SIDE), 2)


def corner(off_ref, j):
    z = lax.div(lax.axis_index("depth"), LANES)
    scan = 2 * j + lax.rem(z, 2)
    return off_ref[scan, 0], off_ref[scan, 1]


def around(scan, z, lane, planes, distance):
    return scan, LANES * lax.rem(z + planes + distance, planes) + lane


def strip_rows(z, rows):
    return pl.ds(pl.multiple_of(turned(z) * rows, 8), rows)


def gather_kernel(
    off_ref, raw, field_ref, corner_ref,
    near_off, made, line, off_sem, turn_sem, line_send, line_recv, send_sem, recv_sem,
):
    scan, z, lane = place()
    groups = lax.axis_size("scan")
    planes = lax.axis_size("depth") // LANES
    rows = made.shape[1]
    rounds = planes // 4
    fetch = pltpu.make_async_copy(off_ref, near_off, off_sem)
    fetch.start()
    to = (turned(z), LANES * turned(scan) + lane)
    stays = turned(z) == scan
    near = (-2, -1, 1, 2)

    barrier = pltpu.get_barrier_semaphore()
    for distance in near:
        pl.semaphore_signal(
            barrier, inc=1, device_id=around(scan, z, lane, planes, distance), device_id_type=MESH)

    @pl.when(jnp.logical_not(stays))
    def _():
        pl.semaphore_signal(barrier, inc=1, device_id=to, device_id_type=MESH)

    def greet(step, carry):
        other = (lax.rem(scan + step, groups), LANES * z + lane)
        pl.semaphore_signal(barrier, inc=1, device_id=other, device_id_type=MESH)
        return carry

    lax.fori_loop(1, groups, greet, 0)
    line[...] = jnp.zeros_like(line)
    field_ref[:, groups * rows :] = jnp.zeros((2, field_ref.shape[1] - groups * rows, field_ref.shape[2]), F32)
    fetch.wait()
    line[:, : near_off.shape[1]] = near_off[...]
    amp = jnp.exp(-raw[1])
    made[0] = amp * jnp.cos(raw[0])
    made[1] = amp * jnp.sin(raw[0])

    def turn(part):
        return pltpu.make_async_remote_copy(
            src_ref=made.at[part], dst_ref=field_ref.at[part, strip_rows(turned(scan), rows), :],
            send_sem=turn_sem.at[0, part], recv_sem=turn_sem.at[1, part], device_id=to, device_id_type=MESH)

    def stay(part):
        return pltpu.make_async_copy(
            made.at[part], field_ref.at[part, strip_rows(z, rows), :], turn_sem.at[1, part])

    @pl.when(stays)
    def _():
        pl.semaphore_wait(barrier, len(near) + groups - 1)
        for part in range(2):
            stay(part).start()

    @pl.when(jnp.logical_not(stays))
    def _():
        pl.semaphore_wait(barrier, len(near) + groups)
        for part in range(2):
            turn(part).start()

    own_line = line.at[pl.ds(lax.div(z, 2), 1), :]
    own = pltpu.make_async_copy(own_line, corner_ref.at[pl.ds(scan, 1), :], line_recv.at[scan])
    own.start()

    def tell(step):
        return pltpu.make_async_remote_copy(
            src_ref=own_line, dst_ref=corner_ref.at[pl.ds(scan, 1), :],
            send_sem=line_send.at[step], recv_sem=line_recv.at[scan],
            device_id=(lax.rem(scan + step, groups), LANES * z + lane), device_id_type=MESH)

    def start_tell(step, carry):
        tell(step).start()
        return carry

    lax.fori_loop(1, groups, start_tell, 0)

    def passing(step, way, distance, part):
        sign = 1 if way == 0 else -1
        whose = lax.rem(z + planes - sign * 2 * step, planes)
        block = field_ref.at[part, strip_rows(whose, rows), :]
        return pltpu.make_async_remote_copy(
            src_ref=block, dst_ref=block,
            send_sem=send_sem.at[way, step, distance - 1, part], recv_sem=recv_sem.at[way, step, distance - 1, part],
            device_id=around(scan, z, lane, planes, sign * distance), device_id_type=MESH)

    def goes(step, way, distance, part):
        return not (way == 1 - part and step == rounds - 1 and distance == 2)

    plan = [(step, way, distance, part)
            for step in range(rounds) for part in range(2) for distance in (2, 1) for way in range(2)
            if goes(step, way, distance, part)]
    for step, way, distance, part in plan:
        if step == 0 and distance == 2 and way == 0:
            stay(part).wait()
        if step > 0 and (distance == 2 or not goes(step, way, 2, part)):
            passing(step - 1, way, 2, part).wait_recv()
        passing(step, way, distance, part).start()
    for part in range(2):
        passing(rounds - 1, part, 2, part).wait_recv()
    for step, way, distance, part in plan:
        if distance == 1:
            passing(step, way, distance, part).wait_recv()
    for step, way, distance, part in plan:
        passing(step, way, distance, part).wait_send()

    @pl.when(jnp.logical_not(stays))
    def _():
        for part in range(2):
            turn(part).wait_send()

    def end_tell(step, carry):
        one = lax.rem(scan + step, groups)
        pltpu.make_async_copy(own_line, corner_ref.at[pl.ds(one, 1), :], line_recv.at[one]).wait()

        @pl.when(step > 0)
        def _():
            tell(step).wait_send()
        return carry

    lax.fori_loop(0, groups, end_tell, 0)


def window_kernel(corner_ref, field_ref, out_ref, off_ref, off_sem):
    win = out_ref.shape[-1]
    fetch = pltpu.make_async_copy(corner_ref, off_ref, off_sem)
    fetch.start()
    fetch.wait()

    def one(j, carry):
        row, col = corner(off_ref, j)
        high = lax.div(row, 8)
        low = row - 8 * high
        side = lax.min(lax.div(col, win), 1)
        tall = pl.ds(pl.multiple_of(8 * high, 8), win + 8)
        wide = pl.ds(pl.multiple_of(win * side, win), 2 * win)
        for part in range(2):
            rows = field_ref[part, tall, wide]
            cols = pltpu.roll(rows, lax.rem(2 * win - (col - win * side), 2 * win), 1)[:, :win]
            out_ref[j, part] = pltpu.roll(cols, lax.rem(win + 8 - low, win + 8), 0)[:win]
        return carry

    lax.fori_loop(0, out_ref.shape[0], one, 0)


def field_kernel(corner_ref, got_ref, out_ref, off_ref, off_sem):
    win = got_ref.shape[-1]
    fetch = pltpu.make_async_copy(corner_ref, off_ref, off_sem)
    fetch.start()
    out_ref[...] = jnp.zeros_like(out_ref)
    fetch.wait()

    def one(j, carry):
        row, col = corner(off_ref, j)
        high = lax.div(row, 8)
        low = row - 8 * high
        side = lax.min(lax.div(col, win), 1)
        tall = pl.ds(pl.multiple_of(8 * high, 8), win + 8)
        wide = pl.ds(pl.multiple_of(win * side, win), 2 * win)
        for part in range(2):
            block = jnp.concatenate([got_ref[j, part], jnp.zeros((8, win), F32)], axis=0)
            block = pltpu.roll(block, low, 0)
            block = jnp.concatenate([block, jnp.zeros((win + 8, win), F32)], axis=1)
            out_ref[part, tall, wide] += pltpu.roll(block, col - win * side, 1)
        return carry

    lax.fori_loop(0, got_ref.shape[0], one, 0)


def chain_kernel(
    sections, num_pos, tw_ref, probe_ref, all_meas_ref, all_tab_ref, got_ref,
    trans, exits, wave, meas_ref, tab_ref, load_sem, go_sem, win_send, win_recv, grad_send, grad_recv,
):
    scan, z, lane = place()
    depth = LANES * z + lane
    mine = 2 * turned(scan) + lane
    slot = lax.div(z, 2)
    member = lax.div(scan, 2)

    def is_home(on_scan, on_lane):
        return jnp.logical_and(lax.rem(on_scan, 2) == lax.rem(z, 2), on_lane == lax.rem(lax.div(on_scan, SIDE), 2))

    active = is_home(scan, lane)

    def owner(k):
        return turned(lax.div(k, LANES)), LANES * z + lax.rem(k, LANES)

    loads = [
        pltpu.make_async_copy(src, dst, load_sem.at[i])
        for i, (src, dst) in enumerate(
            ((probe_ref, wave), (all_meas_ref.at[slot], meas_ref), (all_tab_ref, tab_ref)))
    ]
    for load in loads:
        load.start()
    barrier = pltpu.get_barrier_semaphore()

    @pl.when(active)
    def _():
        def greet(k, carry):
            @pl.when(k != mine)
            def _():
                pl.semaphore_signal(barrier, inc=1, device_id=owner(k), device_id_type=MESH)
            return carry
        lax.fori_loop(0, sections, greet, 0)

    @pl.when(jnp.logical_not(active))
    def _():
        def greet(j, carry):
            pl.semaphore_signal(barrier, inc=1, device_id=home(j, z), device_id_type=MESH)
            return carry
        lax.fori_loop(0, num_pos, greet, 0)

    @pl.when(active)
    def _():
        pl.semaphore_wait(barrier, sections - 1)

    @pl.when(jnp.logical_not(active))
    def _():
        pl.semaphore_wait(barrier, num_pos)

    def is_here(j):
        return jnp.logical_and(active, j == member)

    def window_copy(j):
        return pltpu.make_async_remote_copy(
            src_ref=tw_ref.at[j], dst_ref=trans.at[mine], send_sem=win_send.at[j], recv_sem=win_recv.at[mine],
            device_id=home(j, z), device_id_type=MESH)

    def send_window(step, carry):
        j = lax.rem(step + member, num_pos)
        here = is_here(j)

        @pl.when(jnp.logical_not(here))
        def _():
            window_copy(j).start()

        @pl.when(here)
        def _():
            pltpu.make_async_copy(tw_ref.at[j], trans.at[mine], win_recv.at[mine]).start()
        return carry

    def send_windows():
        lax.fori_loop(0, num_pos, send_window, 0)

    @pl.when(mine < AHEAD)
    def _():
        send_windows()

    @pl.when(jnp.logical_and(jnp.logical_not(active), mine >= AHEAD))
    def _():
        pl.semaphore_wait(go_sem, 1)
        send_windows()

    def call_up(k):
        @pl.when(jnp.logical_and(k == mine, k >= AHEAD))
        def _():
            send_windows()

        to, on_plane = owner(k)
        on_lane = on_plane - LANES * z
        awaits = jnp.logical_not(is_home(to, on_lane))
        chosen = jnp.logical_and(lax.rem(k, num_pos) == member, k < sections)

        @pl.when(jnp.logical_and(awaits, chosen))
        def _():
            pl.semaphore_signal(go_sem, inc=1, device_id=owner(k), device_id_type=MESH)

    def grad_copy(k):
        return pltpu.make_async_remote_copy(
            src_ref=exits.at[k], dst_ref=got_ref.at[member], send_sem=grad_send.at[k],
            recv_sem=grad_recv.at[member], device_id=owner(k), device_id_type=MESH)

    for load in loads:
        load.wait()

    @pl.when(active)
    def _():
        def step_in(k):
            pltpu.make_async_copy(tw_ref.at[0], trans.at[k], win_recv.at[k]).wait()
            tr, ti = trans[k, 0], trans[k, 1]
            wr, wi = wave[0], wave[1]
            er = wr * tr - wi * ti
            ei = wr * ti + wi * tr
            exits[k, 0] = er
            exits[k, 1] = ei
            return er, ei

        def forward(k, carry):
            call_up(k + AHEAD)
            er, ei = step_in(k)
            wr, wi = sandwich(er, ei, tab_ref, 0, 2)
            wave[0] = wr
            wave[1] = wi
            return carry

        lax.fori_loop(0, sections - 1, forward, 0, unroll=8)
        er, ei = step_in(sections - 1)
        fr, fi = sandwich(er, ei, tab_ref, 4, 6)
        resid = fr * fr + fi * fi - meas_ref[...]
        lr, li = sandwich(resid * fr, resid * fi, tab_ref, 6, 4)
        wave[0] = lr
        wave[1] = li

        def grads(k):
            er, ei = exits[k, 0], exits[k, 1]
            lr, li = wave[0], wave[1]
            exits[k, 0] = er * li - ei * lr
            exits[k, 1] = -(er * lr + ei * li)

            @pl.when(k != mine)
            def _():
                grad_copy(k).start()

            @pl.when(k == mine)
            def _():
                pltpu.make_async_copy(exits.at[k], got_ref.at[member], grad_recv.at[member]).start()
            return lr, li

        def backward(j, carry):
            k = sections - 1 - j
            lr, li = grads(k)
            tr, ti = trans[k, 0], trans[k, 1]
            wr, wi = sandwich(tr * lr + ti * li, tr * li - ti * lr, tab_ref, 2, 0)
            wave[0] = wr
            wave[1] = wi
            return carry

        lax.fori_loop(0, sections - 1, backward, 0, unroll=8)
        grads(0)

    def finish(j, carry):
        @pl.when(jnp.logical_not(is_here(j)))
        def _():
            window_copy(j).wait_send()
        pltpu.make_async_copy(tw_ref.at[0], got_ref.at[j], grad_recv.at[j]).wait()
        return carry

    lax.fori_loop(0, num_pos, finish, 0)

    @pl.when(active)
    def _():
        def drain(k, carry):
            @pl.when(k != mine)
            def _():
                grad_copy(k).wait_send()
            return carry
        lax.fori_loop(0, sections, drain, 0)


def sum_kernel(parts_ref, both_ref, got, made, last, turn_sem, send_sem, recv_sem):
    scan, z, lane = place()
    planes = lax.axis_size("depth") // LANES
    rows = last.shape[2]
    rounds = planes // 4
    to = (turned(z), LANES * turned(scan) + lane)
    stays = turned(z) == scan
    near = (-2, -1, 1, 2)
    barrier = pltpu.get_barrier_semaphore()
    for distance in near:
        pl.semaphore_signal(
            barrier, inc=1, device_id=around(scan, z, lane, planes, distance), device_id_type=MESH)

    @pl.when(jnp.logical_not(stays))
    def _():
        pl.semaphore_signal(barrier, inc=1, device_id=to, device_id_type=MESH)
        pl.semaphore_wait(barrier, len(near) + 1)

    @pl.when(stays)
    def _():
        pl.semaphore_wait(barrier, len(near))

    def strip(way, ahead, part):
        sign = 1 if way == 0 else -1
        return parts_ref.at[part, strip_rows(lax.rem(z + planes + sign * ahead, planes), rows), :]

    def goes(step, way, distance, part):
        return not (way == 1 - part and step == 0 and distance == 2)

    def passing(step, way, distance, part):
        ahead = planes // 2 - 2 * step - (2 - distance)
        bare = distance == 1 or step == 0
        return pltpu.make_async_remote_copy(
            src_ref=strip(way, ahead, part) if bare else made.at[way, step - 1, part],
            dst_ref=got.at[way, step, distance - 1, part],
            send_sem=send_sem.at[way, step, distance - 1, part],
            recv_sem=recv_sem.at[way, step, distance - 1, part],
            device_id=around(scan, z, lane, planes, distance if way == 0 else -distance), device_id_type=MESH)

    def arrived(step, way, part):
        passing(step, way, 1, part).wait_recv()
        total = got[way, step, 0, part]
        if goes(step, way, 2, part):
            passing(step, way, 2, part).wait_recv()
            total = total + got[way, step, 1, part]
        return total

    for part in range(2):
        for way in range(2):
            if goes(0, way, 2, part):
                passing(0, way, 2, part).start()
        for way in range(2):
            passing(0, way, 1, part).start()
    for part in range(2):
        for way in range(2):
            passing(1, way, 1, part).start()
    for step in range(1, rounds):
        for part in range(2):
            for way in range(2):
                ahead = planes // 2 - 2 * step
                made[way, step - 1, part] = strip(way, ahead, part)[...] + arrived(step - 1, way, part)
                passing(step, way, 2, part).start()
            if step + 1 < rounds:
                for way in range(2):
                    passing(step + 1, way, 1, part).start()

    def turn(part):
        return pltpu.make_async_remote_copy(
            src_ref=last.at[0, part], dst_ref=last.at[1, part],
            send_sem=turn_sem.at[0, part], recv_sem=turn_sem.at[1, part],
            device_id=to, device_id_type=MESH)

    for part in range(2):
        total = strip(0, 0, part)[...] + (arrived(rounds - 1, 0, part) + arrived(rounds - 1, 1, part))
        last[0, part] = total

        @pl.when(jnp.logical_not(stays))
        def _():
            turn(part).start()

    for part in range(2):
        @pl.when(jnp.logical_not(stays))
        def _():
            turn(part).wait()
            both_ref[part] = last[1, part]

        @pl.when(stays)
        def _():
            both_ref[part] = last[0, part]

    for step in range(rounds):
        for way in range(2):
            for distance in (1, 2):
                for part in range(2):
                    if goes(step, way, distance, part):
                        passing(step, way, distance, part).wait_send()


def shards(tab, phase, absorb, probe, offsets, measured):
    win = probe.shape[-1]
    obj = phase.shape[-1]
    num_pos = offsets.shape[0]
    sections = lax.axis_size("depth")
    vmem = pl.BlockSpec(memory_space=pltpu.VMEM)
    anywhere = pl.BlockSpec(memory_space=pl.ANY)
    limit = 48 * 1024 * 1024
    groups = lax.axis_size("scan")
    rows = obj // groups
    rounds = sections // LANES // 4
    first = lax.axis_index("scan") * rows
    raw = jnp.concatenate([lax.dynamic_slice_in_dim(values, first, rows, axis=1) for values in (phase, absorb)])
    field, corners = pl.pallas_call(
        gather_kernel,
        out_shape=[
            jax.ShapeDtypeStruct((2, obj + 8, obj), F32),
            jax.ShapeDtypeStruct((groups, 128), jnp.int32),
        ],
        in_specs=[anywhere, vmem],
        out_specs=[vmem, vmem],
        scratch_shapes=[
            pltpu.VMEM((num_pos, 2), jnp.int32),
            pltpu.VMEM((2, rows, obj), F32),
            pltpu.VMEM((num_pos, 128), jnp.int32),
            pltpu.SemaphoreType.DMA,
            pltpu.SemaphoreType.DMA((2, 2)),
            pltpu.SemaphoreType.DMA((groups,)),
            pltpu.SemaphoreType.DMA((groups,)),
            pltpu.SemaphoreType.DMA((2, rounds, 2, 2)),
            pltpu.SemaphoreType.DMA((2, rounds, 2, 2)),
        ],
        compiler_params=pltpu.CompilerParams(
            collective_id=2, has_side_effects=True, vmem_limit_bytes=48 * 1024 * 1024),
    )(offsets, raw)
    windows = pl.pallas_call(
        window_kernel,
        out_shape=jax.ShapeDtypeStruct((num_pos, 2, win, win), F32),
        in_specs=[vmem, vmem],
        out_specs=vmem,
        scratch_shapes=[pltpu.SMEM((groups, 128), jnp.int32), pltpu.SemaphoreType.DMA],
        compiler_params=pltpu.CompilerParams(vmem_limit_bytes=limit),
    )(corners, field)
    got = pl.pallas_call(
        functools.partial(chain_kernel, sections, num_pos),
        out_shape=jax.ShapeDtypeStruct((num_pos, 2, win, win), F32),
        in_specs=[vmem, anywhere, anywhere, anywhere],
        out_specs=vmem,
        scratch_shapes=[
            pltpu.VMEM((sections, 2, win, win), F32),
            pltpu.VMEM((sections, 2, win, win), F32),
            pltpu.VMEM((2, win, win), F32),
            pltpu.VMEM((win, win), F32),
            pltpu.VMEM(tab.shape, BF16),
            pltpu.SemaphoreType.DMA((3,)),
            pltpu.SemaphoreType.REGULAR,
            pltpu.SemaphoreType.DMA((num_pos,)),
            pltpu.SemaphoreType.DMA((sections,)),
            pltpu.SemaphoreType.DMA((sections,)),
            pltpu.SemaphoreType.DMA((num_pos,)),
        ],
        compiler_params=pltpu.CompilerParams(
            collective_id=0, has_side_effects=True, vmem_limit_bytes=limit),
    )(windows, probe, measured, tab)
    fields = pl.pallas_call(
        field_kernel,
        out_shape=jax.ShapeDtypeStruct((2, obj + 8, obj), F32),
        in_specs=[vmem, vmem],
        out_specs=vmem,
        scratch_shapes=[pltpu.SMEM((groups, 128), jnp.int32), pltpu.SemaphoreType.DMA],
        compiler_params=pltpu.CompilerParams(vmem_limit_bytes=limit),
    )(corners, got)
    both = pl.pallas_call(
        sum_kernel,
        out_shape=jax.ShapeDtypeStruct((2, rows, obj), F32),
        in_specs=[vmem],
        out_specs=vmem,
        scratch_shapes=[
            pltpu.VMEM((2, rounds, 2, 2, rows, obj), F32),
            pltpu.VMEM((2, rounds - 1, 2, rows, obj), F32),
            pltpu.VMEM((2, 2, rows, obj), F32),
            pltpu.SemaphoreType.DMA((2, 2)),
            pltpu.SemaphoreType.DMA((2, rounds, 2, 2)),
            pltpu.SemaphoreType.DMA((2, rounds, 2, 2)),
        ],
        compiler_params=pltpu.CompilerParams(
            collective_id=1, has_side_effects=True, vmem_limit_bytes=limit),
    )(fields)
    return both[:1], both[1:]


def solution(mesh):
    tab = tables(128)
    in_specs = (
        P("depth", None, None),
        P("depth", None, None),
        P(),
        P("scan", None),
        P("scan", None, None),
    )
    out_specs = (P("depth", "scan", None), P("depth", "scan", None))

    def run(phase, absorb, probe, offsets, measured):
        body = functools.partial(shards, jnp.asarray(tab))
        return jax.shard_map(body, mesh=mesh, in_specs=in_specs, out_specs=out_specs, check_vma=False)(
            phase, absorb, probe, offsets, measured)

    return run
```

```python
import functools

import jax
import jax.numpy as jnp
import ml_dtypes
import numpy as np
from jax import lax
from jax.experimental import pallas as pl
from jax.experimental.pallas import tpu as pltpu
from jax.sharding import PartitionSpec as P

MESH = pl.DeviceIdType.MESH
BF16 = jnp.bfloat16
F32 = jnp.float32
LANES = 2
SIDE = 4
AHEAD = 12


def tables(win):
    idx = np.arange(win)
    ang = 2.0 * np.pi * (np.outer(idx, idx) % win) / win
    fwd = np.exp(-1j * ang) / np.sqrt(win)
    signed = np.where(idx < win // 2, idx, idx - win).astype(np.float64)
    chirp = np.exp(-1j * signed**2 / win)
    prop = np.conj(fwd) @ (chirp[:, None] * fwd)
    prop = 0.5 * (prop + prop.T)
    out = []
    for mat in (prop, fwd):
        right = np.block([[mat.real, mat.imag], [-mat.imag, mat.real]])
        left = np.block([[mat.real, -mat.imag], [mat.imag, mat.real]])
        for block in (right, left):
            block = block.astype(np.float32)
            high = block.astype(ml_dtypes.bfloat16)
            low = (block - high.astype(np.float32)).astype(ml_dtypes.bfloat16)
            out += [high, low]
    return np.stack(out)


def split(values):
    high = values.astype(BF16)
    low = (values - high.astype(F32)).astype(BF16)
    return high, low


def sandwich(re, im, tab, right, left):
    win = re.shape[0]
    high, low = split(jnp.concatenate([re, im], axis=1))
    both = jnp.concatenate([high, low], axis=0)
    main = jnp.dot(both, tab[right], preferred_element_type=F32)
    half = main[:win] + main[win:] + jnp.dot(high, tab[right + 1], preferred_element_type=F32)
    high, low = split(jnp.concatenate([half[:, :win], half[:, win:]], axis=0))
    both = jnp.concatenate([high, low], axis=1)
    main = jnp.dot(tab[left], both, preferred_element_type=F32)
    done = main[:, :win] + main[:, win:] + jnp.dot(tab[left + 1], high, preferred_element_type=F32)
    return done[:win], done[win:]


def turned(index):
    first, last = lax.div(index, 8), lax.rem(index, 2)
    return index + 7 * (last - first)


def place():
    depth = lax.axis_index("depth")
    return lax.axis_index("scan"), lax.div(depth, LANES), lax.rem(depth, LANES)


def home(j, z):
    scan = 2 * j + lax.rem(z, 2)
    return scan, LANES * z + lax.rem(lax.div(scan, SIDE), 2)


def corner(off_ref, j):
    z = lax.div(lax.axis_index("depth"), LANES)
    scan = 2 * j + lax.rem(z, 2)
    return off_ref[scan, 0], off_ref[scan, 1]


def around(scan, z, lane, planes, distance):
    return scan, LANES * lax.rem(z + planes + distance, planes) + lane


def strip_rows(z, rows):
    return pl.ds(pl.multiple_of(turned(z) * rows, 8), rows)


def gather_kernel(
    off_ref, raw, field_ref, corner_ref,
    near_off, made, line, off_sem, turn_sem, line_send, line_recv, send_sem, recv_sem,
):
    scan, z, lane = place()
    groups = lax.axis_size("scan")
    planes = lax.axis_size("depth") // LANES
    rows = made.shape[1]
    rounds = planes // 4
    fetch = pltpu.make_async_copy(off_ref, near_off, off_sem)
    fetch.start()
    to = (turned(z), LANES * turned(scan) + lane)
    stays = turned(z) == scan
    near = (-2, -1, 1, 2)

    barrier = pltpu.get_barrier_semaphore()
    for distance in near:
        pl.semaphore_signal(
            barrier, inc=1, device_id=around(scan, z, lane, planes, distance), device_id_type=MESH)

    @pl.when(jnp.logical_not(stays))
    def _():
        pl.semaphore_signal(barrier, inc=1, device_id=to, device_id_type=MESH)

    def greet(step, carry):
        other = (lax.rem(scan + step, groups), LANES * z + lane)
        pl.semaphore_signal(barrier, inc=1, device_id=other, device_id_type=MESH)
        return carry

    lax.fori_loop(1, groups, greet, 0)
    line[...] = jnp.zeros_like(line)
    field_ref[:, groups * rows :] = jnp.zeros((2, field_ref.shape[1] - groups * rows, field_ref.shape[2]), F32)
    fetch.wait()
    line[:, : near_off.shape[1]] = near_off[...]
    amp = jnp.exp(-raw[1])
    made[0] = amp * jnp.cos(raw[0])
    made[1] = amp * jnp.sin(raw[0])

    def turn(part):
        return pltpu.make_async_remote_copy(
            src_ref=made.at[part], dst_ref=field_ref.at[part, strip_rows(turned(scan), rows), :],
            send_sem=turn_sem.at[0, part], recv_sem=turn_sem.at[1, part], device_id=to, device_id_type=MESH)

    def stay(part):
        return pltpu.make_async_copy(
            made.at[part], field_ref.at[part, strip_rows(z, rows), :], turn_sem.at[1, part])

    @pl.when(stays)
    def _():
        pl.semaphore_wait(barrier, len(near) + groups - 1)
        for part in range(2):
            stay(part).start()

    @pl.when(jnp.logical_not(stays))
    def _():
        pl.semaphore_wait(barrier, len(near) + groups)
        for part in range(2):
            turn(part).start()

    own_line = line.at[pl.ds(lax.div(z, 2), 1), :]
    own = pltpu.make_async_copy(own_line, corner_ref.at[pl.ds(scan, 1), :], line_recv.at[scan])
    own.start()

    def tell(step):
        return pltpu.make_async_remote_copy(
            src_ref=own_line, dst_ref=corner_ref.at[pl.ds(scan, 1), :],
            send_sem=line_send.at[step], recv_sem=line_recv.at[scan],
            device_id=(lax.rem(scan + step, groups), LANES * z + lane), device_id_type=MESH)

    def start_tell(step, carry):
        tell(step).start()
        return carry

    lax.fori_loop(1, groups, start_tell, 0)

    def passing(step, way, distance, part):
        sign = 1 if way == 0 else -1
        whose = lax.rem(z + planes - sign * 2 * step, planes)
        block = field_ref.at[part, strip_rows(whose, rows), :]
        return pltpu.make_async_remote_copy(
            src_ref=block, dst_ref=block,
            send_sem=send_sem.at[way, step, distance - 1, part], recv_sem=recv_sem.at[way, step, distance - 1, part],
            device_id=around(scan, z, lane, planes, sign * distance), device_id_type=MESH)

    def goes(step, way, distance, part):
        return not (way == 1 - part and step == rounds - 1 and distance == 2)

    plan = [(step, way, distance, part)
            for step in range(rounds) for part in range(2) for distance in (2, 1) for way in range(2)
            if goes(step, way, distance, part)]
    for step, way, distance, part in plan:
        if step == 0 and distance == 2 and way == 0:
            stay(part).wait()
        if step > 0 and (distance == 2 or not goes(step, way, 2, part)):
            passing(step - 1, way, 2, part).wait_recv()
        passing(step, way, distance, part).start()
    for part in range(2):
        passing(rounds - 1, part, 2, part).wait_recv()
    for step, way, distance, part in plan:
        if distance == 1:
            passing(step, way, distance, part).wait_recv()
    for step, way, distance, part in plan:
        passing(step, way, distance, part).wait_send()

    @pl.when(jnp.logical_not(stays))
    def _():
        for part in range(2):
            turn(part).wait_send()

    def end_tell(step, carry):
        one = lax.rem(scan + step, groups)
        pltpu.make_async_copy(own_line, corner_ref.at[pl.ds(one, 1), :], line_recv.at[one]).wait()

        @pl.when(step > 0)
        def _():
            tell(step).wait_send()
        return carry

    lax.fori_loop(0, groups, end_tell, 0)


def window_kernel(corner_ref, field_ref, out_ref, off_ref, off_sem):
    win = out_ref.shape[-1]
    fetch = pltpu.make_async_copy(corner_ref, off_ref, off_sem)
    fetch.start()
    fetch.wait()

    def one(j, carry):
        row, col = corner(off_ref, j)
        high = lax.div(row, 8)
        low = row - 8 * high
        side = lax.min(lax.div(col, win), 1)
        tall = pl.ds(pl.multiple_of(8 * high, 8), win + 8)
        wide = pl.ds(pl.multiple_of(win * side, win), 2 * win)
        for part in range(2):
            rows = field_ref[part, tall, wide]
            cols = pltpu.roll(rows, lax.rem(2 * win - (col - win * side), 2 * win), 1)[:, :win]
            out_ref[j, part] = pltpu.roll(cols, lax.rem(win + 8 - low, win + 8), 0)[:win]
        return carry

    lax.fori_loop(0, out_ref.shape[0], one, 0)


def field_kernel(corner_ref, got_ref, out_ref, off_ref, off_sem):
    win = got_ref.shape[-1]
    fetch = pltpu.make_async_copy(corner_ref, off_ref, off_sem)
    fetch.start()
    out_ref[...] = jnp.zeros_like(out_ref)
    fetch.wait()

    def one(j, carry):
        row, col = corner(off_ref, j)
        high = lax.div(row, 8)
        low = row - 8 * high
        side = lax.min(lax.div(col, win), 1)
        tall = pl.ds(pl.multiple_of(8 * high, 8), win + 8)
        wide = pl.ds(pl.multiple_of(win * side, win), 2 * win)
        for part in range(2):
            block = jnp.concatenate([got_ref[j, part], jnp.zeros((8, win), F32)], axis=0)
            block = pltpu.roll(block, low, 0)
            block = jnp.concatenate([block, jnp.zeros((win + 8, win), F32)], axis=1)
            out_ref[part, tall, wide] += pltpu.roll(block, col - win * side, 1)
        return carry

    lax.fori_loop(0, got_ref.shape[0], one, 0)


def chain_kernel(
    sections, num_pos, tw_ref, probe_ref, all_meas_ref, all_tab_ref, got_ref,
    trans, exits, wave, meas_ref, tab_ref, load_sem, go_sem, win_send, win_recv, grad_send, grad_recv,
):
    scan, z, lane = place()
    depth = LANES * z + lane
    mine = 2 * turned(scan) + lane
    slot = lax.div(z, 2)
    member = lax.div(scan, 2)

    def is_home(on_scan, on_lane):
        return jnp.logical_and(lax.rem(on_scan, 2) == lax.rem(z, 2), on_lane == lax.rem(lax.div(on_scan, SIDE), 2))

    active = is_home(scan, lane)

    def owner(k):
        return turned(lax.div(k, LANES)), LANES * z + lax.rem(k, LANES)

    loads = [
        pltpu.make_async_copy(src, dst, load_sem.at[i])
        for i, (src, dst) in enumerate(
            ((probe_ref, wave), (all_meas_ref.at[slot], meas_ref), (all_tab_ref, tab_ref)))
    ]
    for load in loads:
        load.start()
    barrier = pltpu.get_barrier_semaphore()

    @pl.when(active)
    def _():
        def greet(k, carry):
            @pl.when(k != mine)
            def _():
                pl.semaphore_signal(barrier, inc=1, device_id=owner(k), device_id_type=MESH)
            return carry
        lax.fori_loop(0, sections, greet, 0)

    @pl.when(jnp.logical_not(active))
    def _():
        def greet(j, carry):
            pl.semaphore_signal(barrier, inc=1, device_id=home(j, z), device_id_type=MESH)
            return carry
        lax.fori_loop(0, num_pos, greet, 0)

    @pl.when(active)
    def _():
        pl.semaphore_wait(barrier, sections - 1)

    @pl.when(jnp.logical_not(active))
    def _():
        pl.semaphore_wait(barrier, num_pos)

    def is_here(j):
        return jnp.logical_and(active, j == member)

    def window_copy(j):
        return pltpu.make_async_remote_copy(
            src_ref=tw_ref.at[j], dst_ref=trans.at[mine], send_sem=win_send.at[j], recv_sem=win_recv.at[mine],
            device_id=home(j, z), device_id_type=MESH)

    def send_window(step, carry):
        j = lax.rem(step + member, num_pos)
        here = is_here(j)

        @pl.when(jnp.logical_not(here))
        def _():
            window_copy(j).start()

        @pl.when(here)
        def _():
            pltpu.make_async_copy(tw_ref.at[j], trans.at[mine], win_recv.at[mine]).start()
        return carry

    def send_windows():
        lax.fori_loop(0, num_pos, send_window, 0)

    @pl.when(mine < AHEAD)
    def _():
        send_windows()

    @pl.when(jnp.logical_and(jnp.logical_not(active), mine >= AHEAD))
    def _():
        pl.semaphore_wait(go_sem, 1)
        send_windows()

    def call_up(k):
        @pl.when(jnp.logical_and(k == mine, k >= AHEAD))
        def _():
            send_windows()

        to, on_plane = owner(k)
        on_lane = on_plane - LANES * z
        awaits = jnp.logical_not(is_home(to, on_lane))
        chosen = jnp.logical_and(lax.rem(k, num_pos) == member, k < sections)

        @pl.when(jnp.logical_and(awaits, chosen))
        def _():
            pl.semaphore_signal(go_sem, inc=1, device_id=owner(k), device_id_type=MESH)

    def grad_copy(k):
        return pltpu.make_async_remote_copy(
            src_ref=exits.at[k], dst_ref=got_ref.at[member], send_sem=grad_send.at[k],
            recv_sem=grad_recv.at[member], device_id=owner(k), device_id_type=MESH)

    for load in loads:
        load.wait()

    @pl.when(active)
    def _():
        def step_in(k):
            pltpu.make_async_copy(tw_ref.at[0], trans.at[k], win_recv.at[k]).wait()
            tr, ti = trans[k, 0], trans[k, 1]
            wr, wi = wave[0], wave[1]
            er = wr * tr - wi * ti
            ei = wr * ti + wi * tr
            exits[k, 0] = er
            exits[k, 1] = ei
            return er, ei

        def forward(k, carry):
            call_up(k + AHEAD)
            er, ei = step_in(k)
            wr, wi = sandwich(er, ei, tab_ref, 0, 2)
            wave[0] = wr
            wave[1] = wi
            return carry

        lax.fori_loop(0, sections - 1, forward, 0, unroll=4)
        er, ei = step_in(sections - 1)
        fr, fi = sandwich(er, ei, tab_ref, 4, 6)
        resid = fr * fr + fi * fi - meas_ref[...]
        lr, li = sandwich(resid * fr, resid * fi, tab_ref, 6, 4)
        wave[0] = lr
        wave[1] = li

        def grads(k):
            er, ei = exits[k, 0], exits[k, 1]
            lr, li = wave[0], wave[1]
            exits[k, 0] = er * li - ei * lr
            exits[k, 1] = -(er * lr + ei * li)

            @pl.when(k != mine)
            def _():
                grad_copy(k).start()

            @pl.when(k == mine)
            def _():
                pltpu.make_async_copy(exits.at[k], got_ref.at[member], grad_recv.at[member]).start()
            return lr, li

        def backward(j, carry):
            k = sections - 1 - j
            lr, li = grads(k)
            tr, ti = trans[k, 0], trans[k, 1]
            wr, wi = sandwich(tr * lr + ti * li, tr * li - ti * lr, tab_ref, 2, 0)
            wave[0] = wr
            wave[1] = wi
            return carry

        lax.fori_loop(0, sections - 1, backward, 0, unroll=4)
        grads(0)

    def finish(j, carry):
        @pl.when(jnp.logical_not(is_here(j)))
        def _():
            window_copy(j).wait_send()
        pltpu.make_async_copy(tw_ref.at[0], got_ref.at[j], grad_recv.at[j]).wait()
        return carry

    lax.fori_loop(0, num_pos, finish, 0)

    @pl.when(active)
    def _():
        def drain(k, carry):
            @pl.when(k != mine)
            def _():
                grad_copy(k).wait_send()
            return carry
        lax.fori_loop(0, sections, drain, 0)


def sum_kernel(parts_ref, both_ref, got, made, last, turn_sem, send_sem, recv_sem):
    scan, z, lane = place()
    planes = lax.axis_size("depth") // LANES
    rows = last.shape[2]
    rounds = planes // 4
    to = (turned(z), LANES * turned(scan) + lane)
    stays = turned(z) == scan
    near = (-2, -1, 1, 2)
    barrier = pltpu.get_barrier_semaphore()
    for distance in near:
        pl.semaphore_signal(
            barrier, inc=1, device_id=around(scan, z, lane, planes, distance), device_id_type=MESH)

    @pl.when(jnp.logical_not(stays))
    def _():
        pl.semaphore_signal(barrier, inc=1, device_id=to, device_id_type=MESH)
        pl.semaphore_wait(barrier, len(near) + 1)

    @pl.when(stays)
    def _():
        pl.semaphore_wait(barrier, len(near))

    def strip(way, ahead, part):
        sign = 1 if way == 0 else -1
        return parts_ref.at[part, strip_rows(lax.rem(z + planes + sign * ahead, planes), rows), :]

    def goes(step, way, distance, part):
        return not (way == 1 - part and step == 0 and distance == 2)

    def passing(step, way, distance, part):
        ahead = planes // 2 - 2 * step - (2 - distance)
        bare = distance == 1 or step == 0
        return pltpu.make_async_remote_copy(
            src_ref=strip(way, ahead, part) if bare else made.at[way, step - 1, part],
            dst_ref=got.at[way, step, distance - 1, part],
            send_sem=send_sem.at[way, step, distance - 1, part],
            recv_sem=recv_sem.at[way, step, distance - 1, part],
            device_id=around(scan, z, lane, planes, distance if way == 0 else -distance), device_id_type=MESH)

    def arrived(step, way, part):
        passing(step, way, 1, part).wait_recv()
        total = got[way, step, 0, part]
        if goes(step, way, 2, part):
            passing(step, way, 2, part).wait_recv()
            total = total + got[way, step, 1, part]
        return total

    for part in range(2):
        for way in range(2):
            if goes(0, way, 2, part):
                passing(0, way, 2, part).start()
        for way in range(2):
            passing(0, way, 1, part).start()
    for part in range(2):
        for way in range(2):
            passing(1, way, 1, part).start()
    for step in range(1, rounds):
        for part in range(2):
            for way in range(2):
                ahead = planes // 2 - 2 * step
                made[way, step - 1, part] = strip(way, ahead, part)[...] + arrived(step - 1, way, part)
                passing(step, way, 2, part).start()
            if step + 1 < rounds:
                for way in range(2):
                    passing(step + 1, way, 1, part).start()

    def turn(part):
        return pltpu.make_async_remote_copy(
            src_ref=last.at[0, part], dst_ref=last.at[1, part],
            send_sem=turn_sem.at[0, part], recv_sem=turn_sem.at[1, part],
            device_id=to, device_id_type=MESH)

    for part in range(2):
        total = strip(0, 0, part)[...] + (arrived(rounds - 1, 0, part) + arrived(rounds - 1, 1, part))
        last[0, part] = total

        @pl.when(jnp.logical_not(stays))
        def _():
            turn(part).start()

    for part in range(2):
        @pl.when(jnp.logical_not(stays))
        def _():
            turn(part).wait()
            both_ref[part] = last[1, part]

        @pl.when(stays)
        def _():
            both_ref[part] = last[0, part]

    for step in range(rounds):
        for way in range(2):
            for distance in (1, 2):
                for part in range(2):
                    if goes(step, way, distance, part):
                        passing(step, way, distance, part).wait_send()


def shards(tab, phase, absorb, probe, offsets, measured):
    win = probe.shape[-1]
    obj = phase.shape[-1]
    num_pos = offsets.shape[0]
    sections = lax.axis_size("depth")
    vmem = pl.BlockSpec(memory_space=pltpu.VMEM)
    anywhere = pl.BlockSpec(memory_space=pl.ANY)
    limit = 48 * 1024 * 1024
    groups = lax.axis_size("scan")
    rows = obj // groups
    rounds = sections // LANES // 4
    first = lax.axis_index("scan") * rows
    raw = jnp.concatenate([lax.dynamic_slice_in_dim(values, first, rows, axis=1) for values in (phase, absorb)])
    field, corners = pl.pallas_call(
        gather_kernel,
        out_shape=[
            jax.ShapeDtypeStruct((2, obj + 8, obj), F32),
            jax.ShapeDtypeStruct((groups, 128), jnp.int32),
        ],
        in_specs=[anywhere, vmem],
        out_specs=[vmem, vmem],
        scratch_shapes=[
            pltpu.VMEM((num_pos, 2), jnp.int32),
            pltpu.VMEM((2, rows, obj), F32),
            pltpu.VMEM((num_pos, 128), jnp.int32),
            pltpu.SemaphoreType.DMA,
            pltpu.SemaphoreType.DMA((2, 2)),
            pltpu.SemaphoreType.DMA((groups,)),
            pltpu.SemaphoreType.DMA((groups,)),
            pltpu.SemaphoreType.DMA((2, rounds, 2, 2)),
            pltpu.SemaphoreType.DMA((2, rounds, 2, 2)),
        ],
        compiler_params=pltpu.CompilerParams(
            collective_id=2, has_side_effects=True, vmem_limit_bytes=48 * 1024 * 1024),
    )(offsets, raw)
    windows = pl.pallas_call(
        window_kernel,
        out_shape=jax.ShapeDtypeStruct((num_pos, 2, win, win), F32),
        in_specs=[vmem, vmem],
        out_specs=vmem,
        scratch_shapes=[pltpu.SMEM((groups, 128), jnp.int32), pltpu.SemaphoreType.DMA],
        compiler_params=pltpu.CompilerParams(vmem_limit_bytes=limit),
    )(corners, field)
    got = pl.pallas_call(
        functools.partial(chain_kernel, sections, num_pos),
        out_shape=jax.ShapeDtypeStruct((num_pos, 2, win, win), F32),
        in_specs=[vmem, anywhere, anywhere, anywhere],
        out_specs=vmem,
        scratch_shapes=[
            pltpu.VMEM((sections, 2, win, win), F32),
            pltpu.VMEM((sections, 2, win, win), F32),
            pltpu.VMEM((2, win, win), F32),
            pltpu.VMEM((win, win), F32),
            pltpu.VMEM(tab.shape, BF16),
            pltpu.SemaphoreType.DMA((3,)),
            pltpu.SemaphoreType.REGULAR,
            pltpu.SemaphoreType.DMA((num_pos,)),
            pltpu.SemaphoreType.DMA((sections,)),
            pltpu.SemaphoreType.DMA((sections,)),
            pltpu.SemaphoreType.DMA((num_pos,)),
        ],
        compiler_params=pltpu.CompilerParams(
            collective_id=0, has_side_effects=True, vmem_limit_bytes=limit),
    )(windows, probe, measured, tab)
    fields = pl.pallas_call(
        field_kernel,
        out_shape=jax.ShapeDtypeStruct((2, obj + 8, obj), F32),
        in_specs=[vmem, vmem],
        out_specs=vmem,
        scratch_shapes=[pltpu.SMEM((groups, 128), jnp.int32), pltpu.SemaphoreType.DMA],
        compiler_params=pltpu.CompilerParams(vmem_limit_bytes=limit),
    )(corners, got)
    both = pl.pallas_call(
        sum_kernel,
        out_shape=jax.ShapeDtypeStruct((2, rows, obj), F32),
        in_specs=[vmem],
        out_specs=vmem,
        scratch_shapes=[
            pltpu.VMEM((2, rounds, 2, 2, rows, obj), F32),
            pltpu.VMEM((2, rounds - 1, 2, rows, obj), F32),
            pltpu.VMEM((2, 2, rows, obj), F32),
            pltpu.SemaphoreType.DMA((2, 2)),
            pltpu.SemaphoreType.DMA((2, rounds, 2, 2)),
            pltpu.SemaphoreType.DMA((2, rounds, 2, 2)),
        ],
        compiler_params=pltpu.CompilerParams(
            collective_id=1, has_side_effects=True, vmem_limit_bytes=limit),
    )(fields)
    return both[:1], both[1:]


def solution(mesh):
    tab = tables(128)
    in_specs = (
        P("depth", None, None),
        P("depth", None, None),
        P(),
        P("scan", None),
        P("scan", None, None),
    )
    out_specs = (P("depth", "scan", None), P("depth", "scan", None))

    def run(phase, absorb, probe, offsets, measured):
        body = functools.partial(shards, jnp.asarray(tab))
        return jax.shard_map(body, mesh=mesh, in_specs=in_specs, out_specs=out_specs, check_vma=False)(
            phase, absorb, probe, offsets, measured)

    return run
```
